512 devices in a mesh: ctx: 64 (over y, x, core), fsdp: 8 (over z).
Axes of the slice: x: 4, y: 8, z: 8, core: 2. Of those that a mesh axis runs over, the one named last changes fastest.
Arguments:
- query_in: bfloat16 [8, 16384, 768], P('fsdp', 'ctx'), may hold values from -6 to 6
- key_in: bfloat16 [8, 16384, 768], P('fsdp', 'ctx'), may hold values from -6 to 6
- value_in: bfloat16 [8, 16384, 768], P('fsdp', 'ctx'), may hold values from -6 to 6
- out_grad: bfloat16 [8, 16384, 768], P('fsdp', 'ctx'), may hold values from -6 to 6
- w_out: bfloat16 [768, 768], P('fsdp'), may hold values from -0.21875 to 0.21875
- head_offsets: int32 [2, 12], replicated, may hold values from 0 to 1, as said below
- valid_tiles: int32 [8], P('fsdp'), may hold values from 4096 to 16384
Outputs:
- query_gradient: bfloat16 [8, 16384, 768], P('fsdp', 'ctx')
- key_gradient: bfloat16 [8, 16384, 768], P('fsdp', 'ctx')
- value_gradient: bfloat16 [8, 16384, 768], P('fsdp', 'ctx')
The draws below stay inside these ranges and needn't reach their ends.
Inputs may be any that keep to these rules, and one draw needn't show every extreme that they name: head_offsets[b, h] lies below 2^b for every branch b.
All inputs are finite; a program needn't handle non-finite values.
Results may differ from the reference program's by a relative error of at most 0.012.
Values may be sent and summed in bfloat16 or wider, within the bound.
A program may use at most 128 MiB of HBM per device.

```python
import jax
import jax.numpy as jnp
from jax import lax

HEAD_COUNT = 12
D = 768
NB = 2
BRANCH_ROWS = 1024
SLIDE_TILES = 16384
SLIDES = 8


def draw_query_in(key, part):
    key = jax.random.fold_in(key, 11)
    values = jnp.clip(jax.random.normal(key, (SLIDES, SLIDE_TILES, D), jnp.float32), -4.0, 4.0)
    return values.astype(jnp.bfloat16)


def draw_key_in(key, part):
    key = jax.random.fold_in(key, 12)
    values = jnp.clip(jax.random.normal(key, (SLIDES, SLIDE_TILES, D), jnp.float32), -4.0, 4.0)
    return values.astype(jnp.bfloat16)


def draw_head_offsets(key, part):
    key = jax.random.fold_in(key, 13)
    raw = jax.random.randint(key, (NB, HEAD_COUNT), 0, 2 ** (NB - 1), dtype=jnp.int32)
    rates = 2 ** jnp.arange(NB, dtype=jnp.int32)
    head_shifts = raw % rates[:, None]
    chosen = jax.random.randint(jax.random.fold_in(key, 1), (), 0, HEAD_COUNT, dtype=jnp.int32)
    corner = (jnp.arange(NB, dtype=jnp.int32)[:, None] == NB - 1) & (jnp.arange(HEAD_COUNT, dtype=jnp.int32)[None, :] == chosen)
    return jnp.where(corner, 2 ** (NB - 1) - 1, head_shifts).astype(jnp.int32)


def touch_ends(values, rng, least, largest):
    dims = values.shape
    index_at = [jax.random.randint(jax.random.fold_in(rng, axis), (), 0, dims[axis]) for axis in range(len(dims))]
    values = values.at[tuple(index_at)].set(least)
    longest = dims.index(max(dims))
    index_at[longest] = (index_at[longest] + 1) % dims[longest]
    return values.at[tuple(index_at)].set(largest)


def level_of(own_key, shape, split, low, high):
    gain = 1.0
    for axis_at, blocks in split:
        heights = jax.random.uniform(jax.random.fold_in(jax.random.fold_in(own_key, 6), axis_at), (blocks,), jnp.float32, low / len(split), high / len(split))
        gain = gain * jnp.repeat(jnp.exp(heights), shape[axis_at] // blocks).reshape((-1,) + (1,) * (len(shape) - 1 - axis_at))
    return gain


def gaussian(own_key, extent, deviation, limit, pieces=(), kind=jnp.bfloat16):
    loudness = level_of(own_key, extent, pieces, -0.22, 0.18) if pieces else 1.0
    values = jax.random.normal(own_key, extent, jnp.float32) * deviation * loudness
    return jnp.minimum(jnp.maximum(values, -limit), limit).astype(kind)


def setup_inputs(seed: int = 0) -> dict:
    key_of = jax.random.split(jax.random.key(seed), 8)
    return {
        "query_in": draw_query_in(jax.random.fold_in(key_of[7], 71), 0),
        "key_in": draw_key_in(jax.random.fold_in(key_of[7], 71), 0),
        "value_in": gaussian(key_of[2], (SLIDES, SLIDE_TILES, D), 1.0, 6.0, ((0, 8), (1, 64))),
        "out_grad": gaussian(key_of[3], (SLIDES, SLIDE_TILES, D), 1.0, 6.0, ((0, 8), (1, 64))),
        "w_out": gaussian(key_of[4], (D, D), D ** -0.5, 0.21875, ((0, 8),)),
        "head_offsets": draw_head_offsets(jax.random.fold_in(key_of[7], 71), 0),
        "valid_tiles": touch_ends(jax.random.randint(key_of[6], (SLIDES,), SLIDE_TILES // 4, SLIDE_TILES + 1), jax.random.fold_in(key_of[6], 1), SLIDE_TILES // 4, SLIDE_TILES).astype(jnp.int32),
    }


def compact_rows(source_array, dilation_rate, head_shift):
    reshaped_rows = source_array.reshape(SLIDE_TILES // dilation_rate, dilation_rate, source_array.shape[-1])
    picked_rows = (jnp.arange(dilation_rate, dtype=jnp.int32) == head_shift)[None, :, None]
    return jnp.sum(jnp.where(picked_rows, reshaped_rows, 0.0), axis=1)


def expand_rows(row_indices, dilation_rate, head_shift, fill_value):
    picked_rows = (jnp.arange(dilation_rate, dtype=jnp.int32) == head_shift)[None, :, None]
    return jnp.where(picked_rows, row_indices[:, None, :], fill_value).reshape(SLIDE_TILES, row_indices.shape[-1])


def head_grads(inputs, valid_count):
    query_matrix, key, value_matrix, output_gradient, head_shifts = inputs
    head_width = query_matrix.shape[-1]
    logit_scale = head_width ** -0.5
    branch_list = []
    overall_maximum = jnp.full((SLIDE_TILES, 1), -jnp.inf, jnp.float32)
    for branch_index in range(NB):
        dilation_rate = 2 ** branch_index
        head_shift = head_shifts[branch_index]
        segment_count = SLIDE_TILES // (BRANCH_ROWS * dilation_rate)
        branch_parts = [compact_rows(source_array, dilation_rate, head_shift).reshape(segment_count, BRANCH_ROWS, head_width) for source_array in (query_matrix, key, value_matrix, output_gradient)]
        branch_position = (jnp.arange(SLIDE_TILES // dilation_rate, dtype=jnp.int32) * dilation_rate + head_shift).reshape(segment_count, BRANCH_ROWS)
        usable_rows = (branch_position[:, None, :] < valid_count) | (branch_position[:, :, None] >= valid_count)
        attention_scores = jnp.einsum("sid,sjd->sij", branch_parts[0], branch_parts[1]) * logit_scale
        row_maximum = jnp.max(jnp.where(usable_rows, attention_scores, -jnp.inf), axis=-1)
        overall_maximum = jnp.maximum(overall_maximum, expand_rows(row_maximum.reshape(-1, 1), dilation_rate, head_shift, -jnp.inf))
        branch_list.append((dilation_rate, head_shift, branch_parts, usable_rows, attention_scores))
    exponent_sum = jnp.zeros((SLIDE_TILES, 1), jnp.float32)
    for dilation_rate, head_shift, branch_parts, usable_rows, attention_scores in branch_list:
        branch_maximum = compact_rows(overall_maximum, dilation_rate, head_shift).reshape(attention_scores.shape[0], BRANCH_ROWS)
        gradient_terms = jnp.sum(jnp.where(usable_rows, jnp.exp(attention_scores - branch_maximum[..., None]), 0.0), axis=-1)
        exponent_sum = exponent_sum + expand_rows(gradient_terms.reshape(-1, 1), dilation_rate, head_shift, 0.0)
    log_normalizer = overall_maximum + jnp.log(exponent_sum)
    attention_output = jnp.zeros((SLIDE_TILES, head_width), jnp.float32)
    probability_list = []
    for dilation_rate, head_shift, branch_parts, usable_rows, attention_scores in branch_list:
        branch_logsumexp = compact_rows(log_normalizer, dilation_rate, head_shift).reshape(attention_scores.shape[0], BRANCH_ROWS)
        probabilities = jnp.where(usable_rows, jnp.exp(attention_scores - branch_logsumexp[..., None]), 0.0).astype(jnp.bfloat16)
        probability_list.append(probabilities)
        attention_output = attention_output + expand_rows(jnp.einsum("vmx,vxo->vmo", probabilities.astype(jnp.float32), branch_parts[2]).reshape(-1, head_width), dilation_rate, head_shift, 0.0)
    delta_rowsum = jnp.sum(output_gradient * attention_output, axis=-1, keepdims=True)
    query_gradient = jnp.zeros((SLIDE_TILES, head_width), jnp.float32)
    key_gradient = jnp.zeros((SLIDE_TILES, head_width), jnp.float32)
    value_gradient = jnp.zeros((SLIDE_TILES, head_width), jnp.float32)
    for (dilation_rate, head_shift, branch_parts, usable_rows, attention_scores), probabilities in zip(branch_list, probability_list):
        delta_branch = compact_rows(delta_rowsum, dilation_rate, head_shift).reshape(attention_scores.shape[0], BRANCH_ROWS)
        dprob = jnp.einsum("sid,sjd->sij", branch_parts[3], branch_parts[2])
        score_gradient = (probabilities.astype(jnp.float32) * (dprob - delta_branch[..., None])).astype(jnp.bfloat16).astype(jnp.float32)
        query_gradient = query_gradient + expand_rows((jnp.einsum("vmx,vxo->vmo", score_gradient, branch_parts[1]) * logit_scale).reshape(-1, head_width), dilation_rate, head_shift, 0.0)
        key_gradient = key_gradient + expand_rows((jnp.einsum("hab,haw->hbw", score_gradient, branch_parts[0]) * logit_scale).reshape(-1, head_width), dilation_rate, head_shift, 0.0)
        value_gradient = value_gradient + expand_rows(jnp.einsum("hab,haw->hbw", probabilities.astype(jnp.float32), branch_parts[3]).reshape(-1, head_width), dilation_rate, head_shift, 0.0)
    return (query_gradient, key_gradient, value_gradient)


def slide_grads(query_in, key_in, value_in, out_grad, valid_count, w_out, head_offsets):
    head_width = D // HEAD_COUNT
    positions = jnp.arange(SLIDE_TILES, dtype=jnp.int32)
    proj_grad = jnp.dot(out_grad, w_out.T, preferred_element_type=jnp.float32)
    attn_grad = jnp.where((positions < valid_count)[:, None], proj_grad, 0.0).astype(jnp.bfloat16)
    sources = [tensor.astype(jnp.float32).reshape(SLIDE_TILES, HEAD_COUNT, head_width).transpose(1, 0, 2) for tensor in (query_in, key_in, value_in, attn_grad)]

    def one_head(inputs):
        return head_grads(inputs, valid_count)

    results = lax.map(one_head, (sources[0], sources[1], sources[2], sources[3], head_offsets.T))
    return tuple(result.transpose(1, 0, 2).reshape(SLIDE_TILES, D).astype(jnp.bfloat16) for result in results)


def reference(query_in, key_in, value_in, out_grad, w_out, head_offsets, valid_tiles):
    def one_slide(inputs):
        return slide_grads(inputs[0], inputs[1], inputs[2], inputs[3], inputs[4], w_out, head_offsets)

    results = lax.map(one_slide, (query_in, key_in, value_in, out_grad, valid_tiles))
    return (results[0], results[1], results[2])
```

```python
import jax
import jax.numpy as jnp
from jax import lax
from jax.experimental import pallas as pl
from jax.experimental.pallas import tpu as pltpu
from jax.sharding import PartitionSpec as P

HEADS = 12
HD = 64
GROUP = 8
ROWS = 256
HALF = 128
QUAD = GROUP // 2
SEG = GROUP * HALF
QB = 256
KC = 512
SUB = 256
NEG = -1e30
F32 = jnp.float32
BF16 = jnp.bfloat16
MESH = pl.DeviceIdType.MESH


def nt(a, b):
    return lax.dot_general(a, b, (((1,), (1,)), ((), ())), preferred_element_type=F32)


def nn(a, b):
    return jnp.dot(a, b, preferred_element_type=F32)


def row_perm(value):
    r = lax.broadcasted_iota(jnp.int32, (ROWS, ROWS), 0)
    c = lax.broadcasted_iota(jnp.int32, (ROWS, ROWS), 1)
    pos = jnp.where(r < HALF, 2 * r, 2 * r - (ROWS - 1))
    return jnp.where(c == pos, value, 0.0).astype(BF16)


def row_unperm():
    r = lax.broadcasted_iota(jnp.int32, (ROWS, ROWS), 1)
    c = lax.broadcasted_iota(jnp.int32, (ROWS, ROWS), 0)
    pos = jnp.where(r < HALF, 2 * r, 2 * r - (ROWS - 1))
    return jnp.where(c == pos, 1.0, 0.0).astype(BF16)


def kernel(
    q_ref, k_ref, v_ref, og_ref, w_ref, off_ref, valid_ref,
    dq_ref, dk_ref, dv_ref,
    qks, vds, qk, vd, kp, kt, w4, sbuf, dpbuf, dsp, acc, xsib, out, back, perm_og,
    w_send, w_recv, wf_send, wf_recv, a_send, a_recv, f_send, f_recv, x_send, x_recv, o_send, o_recv, l_sem,
):
    ctx = lax.axis_index("ctx")
    z = lax.axis_index("fsdp")
    nz = lax.axis_size("fsdp")
    m = ctx % GROUP
    base = ctx - m
    chip = m // 2
    core = m % 2
    half = m // QUAD
    valid = valid_ref[0]

    def dev(member):
        return (base + member, z)

    def remote(src, dst, ssem, rsem, to):
        return pltpu.make_async_remote_copy(
            src_ref=src, dst_ref=dst, send_sem=ssem, recv_sem=rsem, device_id=to, device_id_type=MESH
        )

    def full_head(p):
        return 3 * (p // 2) + 2 * (p % 2)

    barrier = pltpu.get_barrier_semaphore()
    for d in range(1, GROUP):
        pl.semaphore_signal(barrier, inc=1, device_id=dev(m ^ d), device_id_type=MESH)
    for d in range(1, nz):
        pl.semaphore_signal(barrier, inc=1, device_id=(ctx, (z + d) % nz), device_id_type=MESH)
    pl.semaphore_wait(barrier, GROUP - 1 + nz - 1)

    def w_copy(d):
        return remote(w_ref.at[core], w4.at[z, core], w_send.at[d], w_recv.at[d], (ctx, (z + d) % nz))

    def w_forward(d, c):
        frm = (z + nz - d) % nz
        return remote(w4.at[frm, c], w4.at[frm, c], wf_send.at[d], wf_recv.at[d], dev(m ^ 1))

    for d in range(1, nz):
        w_copy(d).start()
    own_w = pltpu.make_async_copy(w_ref.at[core], w4.at[z, core], l_sem.at[0])
    own_w.start()

    lane = lax.broadcasted_iota(jnp.int32, (HALF, 2 * HD), 1)
    low = lane < HD

    def takes_odd(tile):
        return jnp.where(low, off_ref[1, 2 * tile], off_ref[1, 2 * tile + 1]) == 1

    def pack(dst, left, right, tile):
        odd = takes_odd(tile)
        for s in range(2):
            a, b = (left[HALF:], left[:HALF]) if s == 0 else (left[:HALF], left[HALF:])
            l = jnp.where(odd, a, b)
            a, b = (right[HALF:], right[:HALF]) if s == 0 else (right[:HALF], right[HALF:])
            r = jnp.where(odd, a, b)
            dst[2 * tile, s] = jnp.where(low, l, pltpu.roll(r, HD, 1)).astype(BF16)
            dst[2 * tile + 1, s] = jnp.where(low, pltpu.roll(l, HD, 1), r).astype(BF16)

    def full_copy(src, dst, which, d):
        p = m ^ d
        return remote(
            src.at[full_head(p)], dst.at[0, :, m], a_send.at[which, 0, d], a_recv.at[which, 0, d], dev(p)
        )

    def shared_copy(src, dst, which, dx):
        to = chip ^ dx
        return remote(
            src.at[3 * to + 1], dst.at[1, :, m], a_send.at[which, 1, dx], a_recv.at[which, 1, m % QUAD],
            dev(2 * to + half),
        )

    def local_full(src, dst, which):
        return pltpu.make_async_copy(src.at[full_head(m)], dst.at[0, :, m], l_sem.at[1 + which])

    def local_shared(src, dst, which):
        return pltpu.make_async_copy(src.at[3 * chip + 1], dst.at[1, :, m], l_sem.at[3 + which])

    def exchange(src, dst, which):
        for d in range(1, GROUP):
            full_copy(src, dst, which, d).start()
        local_full(src, dst, which).start()
        for dx in range(1, QUAD):
            shared_copy(src, dst, which, dx).start()

        @pl.when(core != half)
        def _():
            shared_copy(src, dst, which, 0).start()

        @pl.when(core == half)
        def _():
            local_shared(src, dst, which).start()

    def wait_full(src, dst, which):
        local_full(src, dst, which).wait()
        for d in range(1, GROUP):
            remote(
                src.at[0], dst.at[0, :, m ^ d], a_send.at[which, 0, d], a_recv.at[which, 0, d], dev(m ^ d)
            ).wait_recv()

    def wait_shared(src, dst, which):
        for j in range(QUAD):
            s = QUAD * core + j

            @pl.when(s != m)
            def _():
                remote(
                    src.at[0], dst.at[1, :, s], a_send.at[which, 1, 0], a_recv.at[which, 1, j], dev(s)
                ).wait_recv()

        @pl.when(core == half)
        def _():
            local_shared(src, dst, which).wait()

    perm = row_perm(1.0)
    perm_q = row_perm(HD ** -0.5)
    for t in range(HEADS // 2):
        cols = slice(t * 128, (t + 1) * 128)
        pack(qks, nn(perm_q, q_ref[:, cols]), nn(perm, k_ref[:, cols]), t)
    exchange(qks, qk, 0)

    perm_og[...] = nn(perm, og_ref[...]).astype(BF16)

    for d in range(1, nz):
        frm = (z + nz - d) % nz
        remote(w_ref.at[core], w4.at[frm, core], w_send.at[d], w_recv.at[d], (ctx, frm)).wait_recv()
        w_forward(d, core).start()
    own_w.wait()
    w_forward(0, core).start()
    for d in range(nz):
        w_forward(d, 1 - core).wait_recv()
    grad = nt(perm_og[...], w4[...].reshape(HEADS * HD, HEADS * HD))
    r = lax.broadcasted_iota(jnp.int32, (ROWS, 1), 0)
    position = ctx * ROWS + jnp.where(r < HALF, 2 * r, 2 * r - (ROWS - 1))
    grad = jnp.where(position < valid, grad, 0.0)
    for t in range(HEADS // 2):
        cols = slice(t * 128, (t + 1) * 128)
        pack(vds, nn(perm, v_ref[:, cols]), grad[:, cols], t)
    exchange(vds, vd, 1)

    acc[...] = jnp.zeros_like(acc)

    def positions(row, cls, off):
        return base * ROWS + 2 * row + (off if cls == 0 else 1 - off)

    wide = lax.broadcasted_iota(jnp.int32, (KC, 2 * HD), 1)
    key_row = lax.broadcasted_iota(jnp.int32, (KC, 1), 0)

    def prepare(slot, cls, seg, off):
        bias = jnp.where(positions(seg * KC + key_row, cls, off) < valid, 0.0, NEG)
        x = qk[slot, cls, pl.ds(seg * QUAD, QUAD)].reshape(KC, 2 * HD).astype(F32)
        rows = pl.ds(pl.multiple_of(seg * KC, KC), KC)
        kp[slot, cls, rows] = jnp.where(wide >= HD, x, jnp.where(wide == 0, bias, 0.0)).astype(BF16)
        kt[slot, cls, :, rows] = jnp.transpose(x)[HD:].astype(BF16)

    qlane = lax.broadcasted_iota(jnp.int32, (QB, 2 * HD), 1)
    qlow = qlane < HD
    qrow = lax.broadcasted_iota(jnp.int32, (QB, 1), 0)

    def fold(x, op):
        return op(x.reshape(SUB // 8, 8, QB), axis=0)

    def block(slot, off, c, i):
        r0 = pl.multiple_of(c * KC + i * QB, QB)
        s0 = c * QUAD + 2 * i
        parts = []
        for cls in range(2):
            xq = qk[slot, cls, pl.ds(s0, 2)].reshape(QB, 2 * HD).astype(F32)
            xv = vd[slot, cls, pl.ds(s0, 2)].reshape(QB, 2 * HD).astype(F32)
            use = jnp.where(positions(r0 + qrow, cls, off) < valid, 1.0, 0.0)
            qp = jnp.where(qlow, jnp.where(qlane == 0, use, 0.0), pltpu.roll(xq, HD, 1)).astype(BF16)
            gp = jnp.where(qlow, 0.0, xv)
            g0 = gp.astype(BF16)
            gp = pltpu.roll(gp, HD, 1).astype(BF16)
            q0 = jnp.where(qlow, xq, 0.0).astype(BF16)
            grads = jnp.concatenate([q0, g0], axis=0)
            if cls == 0:
                chunks = [(0, c, 2), (0, 1 - c, 1), (1, c, 1)]
            else:
                chunks = [(0, c, 1), (1, c, 1)]
            subs = [(n, kc, seg, mult, u) for n, (kc, seg, mult) in enumerate(chunks) for u in range(KC // SUB)]
            top = jnp.full((8, QB), -jnp.inf, F32)
            for n, kc, seg, mult, u in subs:
                s = nt(kp[slot, kc, pl.ds(pl.multiple_of(seg * KC + u * SUB, SUB), SUB)], qp)
                sbuf[n, u * SUB:(u + 1) * SUB] = s
                top = jnp.maximum(top, fold(s, jnp.max))
            top = jnp.max(top, axis=0, keepdims=True)
            total = jnp.zeros((8, QB), F32)
            dot_sum = jnp.zeros((8, QB), F32)
            for n, kc, seg, mult, u in subs:
                su = slice(u * SUB, (u + 1) * SUB)
                per = SUB // HALF
                values = vd[slot, kc, pl.ds(seg * QUAD + u * per, per)].reshape(SUB, 2 * HD)
                dp = nt(values, gp)
                e = jnp.exp(sbuf[n, su] - top)
                sbuf[n, su] = e
                dpbuf[n, su] = dp
                total = total + mult * fold(e, jnp.sum)
                dot_sum = dot_sum + mult * fold(e * dp, jnp.sum)
            inv = 1.0 / jnp.sum(total, axis=0, keepdims=True)
            delta = jnp.sum(dot_sum, axis=0, keepdims=True) * inv
            dqt = jnp.zeros((HD, QB), F32)
            for n, (kc, seg, mult) in enumerate(chunks):
                rows = pl.ds(pl.multiple_of(seg * KC, KC), KC)
                for u in range(KC // SUB):
                    su = slice(u * SUB, (u + 1) * SUB)
                    p = sbuf[n, su] * inv
                    ds = p * (dpbuf[n, su] - delta)
                    dsp[cls, n, su, :QB] = ds.astype(BF16)
                    dsp[cls, n, su, QB:] = p.astype(BF16)
                acc[slot, kc, rows] += nn(dsp[cls, n], grads * mult if mult != 1 else grads)
                keys_t = kt[slot, kc, :, rows]
                dqt = dqt + nn(keys_t * mult if mult != 1 else keys_t, dsp[cls, n, :, :QB])
            parts.append(dqt)
        dq = jnp.transpose(jnp.concatenate(parts, axis=0)) * (HD ** -0.5)
        out[slot, pl.ds(s0, 2), 2] = dq.reshape(2, HALF, 2 * HD).astype(BF16)

    off0 = off_ref[1, full_head(m)]
    wait_full(qks, qk, 0)
    for cls in range(2):
        for seg in range(2):
            prepare(0, cls, seg, off0)
    wait_full(vds, vd, 1)

    @pl.loop(0, 4)
    def _(t):
        block(0, off0, t // 2, t % 2)

    for cls in range(2):
        out[0, :, cls] = acc[0, cls].reshape(GROUP, HALF, 2 * HD).astype(BF16)

    def out_full(d):
        p = m ^ d
        return remote(out.at[0, p], back.at[full_head(m)], o_send.at[0, d], o_recv.at[0, d], dev(p))

    for d in range(1, GROUP):
        out_full(d).start()
    own_full = pltpu.make_async_copy(out.at[0, m], back.at[full_head(m)], l_sem.at[5])
    own_full.start()

    off1 = off_ref[1, 3 * chip + 1]
    mine = pl.ds(QUAD * core, QUAD)
    theirs = pl.ds(QUAD * (1 - core), QUAD)

    def pass_on(dst, which, part):
        return remote(dst.at[1, 0, part], dst.at[1, 0, part], f_send.at[which], f_recv.at[which], dev(m ^ 1))

    for which, (src, dst) in enumerate(((qks, qk), (vds, vd))):
        wait_shared(src, dst, which)
        pass_on(dst, which, mine).start()
    for which, dst in enumerate((qk, vd)):
        pass_on(dst, which, theirs).wait_recv()
    prepare(1, 0, 0, off1)
    prepare(1, 0, 1, off1)
    prepare(1, 1, core, off1)

    @pl.loop(0, 2)
    def _(t):
        block(1, off1, core, t)

    def swap_terms(c):
        rows = pl.ds(pl.multiple_of(c * KC, KC), KC)
        return remote(acc.at[1, 0, rows], xsib, x_send.at[0], x_recv.at[0], dev(m ^ 1))

    swap_terms(1 - core).start()
    own_rows = pl.ds(pl.multiple_of(core * KC, KC), KC)
    out[1, mine, 1] = acc[1, 1, own_rows].reshape(QUAD, HALF, 2 * HD).astype(BF16)
    swap_terms(core).wait_recv()
    out[1, mine, 0] = (acc[1, 0, own_rows] + xsib[...]).reshape(QUAD, HALF, 2 * HD).astype(BF16)

    def out_shared(j):
        s = QUAD * core + j
        return remote(
            out.at[1, s], back.at[3 * chip + 1], o_send.at[1, j], o_recv.at[1, chip], dev(s)
        )

    own_shared = pltpu.make_async_copy(out.at[1, m], back.at[3 * chip + 1], l_sem.at[6])
    for j in range(QUAD):
        @pl.when(QUAD * core + j != m)
        def _():
            out_shared(j).start()

    @pl.when(core == half)
    def _():
        own_shared.start()

    own_full.wait()
    for d in range(1, GROUP):
        p = m ^ d
        remote(out.at[0, p], back.at[full_head(p)], o_send.at[0, d], o_recv.at[0, d], dev(p)).wait_recv()

    @pl.when(core == half)
    def _():
        own_shared.wait()

    for x in range(QUAD):
        @pl.when(2 * x + half != m)
        def _():
            remote(
                out.at[1, 0], back.at[3 * x + 1], o_send.at[1, 0], o_recv.at[1, x], dev(2 * x + half)
            ).wait_recv()

    unperm = row_unperm()
    for t in range(HEADS // 2):
        cols = slice(t * 128, (t + 1) * 128)
        odd = takes_odd(t)

        def put(ref, sel, oth):
            rows = jnp.concatenate([jnp.where(odd, oth, sel), jnp.where(odd, sel, oth)], axis=0)
            ref[:, cols] = nn(unperm, rows.astype(BF16)).astype(BF16)

        first = [back[2 * t, n].astype(F32) for n in range(3)]
        second = [back[2 * t + 1, n].astype(F32) for n in range(3)]
        left = [jnp.where(low, first[n], pltpu.roll(second[n], HD, 1)) for n in range(3)]
        right = [jnp.where(low, pltpu.roll(first[n], HD, 1), second[n]) for n in range(3)]
        put(dk_ref, left[0], left[1])
        put(dv_ref, right[0], right[1])
        put(dq_ref, left[2], right[2])

    for d in range(1, nz):
        w_copy(d).wait_send()
    for d in range(nz):
        w_forward(d, core).wait_send()
    for which, (src, dst) in enumerate(((qks, qk), (vds, vd))):
        for d in range(1, GROUP):
            full_copy(src, dst, which, d).wait_send()
        for dx in range(1, QUAD):
            shared_copy(src, dst, which, dx).wait_send()

        @pl.when(core != half)
        def _():
            shared_copy(src, dst, which, 0).wait_send()
        pass_on(dst, which, mine).wait_send()
    for d in range(1, GROUP):
        out_full(d).wait_send()
    swap_terms(1 - core).wait_send()
    for j in range(QUAD):
        @pl.when(QUAD * core + j != m)
        def _():
            out_shared(j).wait_send()


def on_device(query_in, key_in, value_in, out_grad, w_out, head_offsets, valid_tiles):
    width = HEADS * HD
    nz = lax.axis_size("fsdp")
    w_rows = w_out.shape[0] // 2
    spec = jax.ShapeDtypeStruct((ROWS, width), BF16)
    vmem = pl.BlockSpec(memory_space=pltpu.VMEM)
    smem = pl.BlockSpec(memory_space=pltpu.SMEM)
    dma = pltpu.SemaphoreType.DMA
    outs = pl.pallas_call(
        kernel,
        out_shape=[spec] * 3,
        in_specs=[vmem] * 5 + [smem] * 2,
        out_specs=[vmem] * 3,
        scratch_shapes=[
            pltpu.VMEM((HEADS, 2, HALF, 2 * HD), BF16),
            pltpu.VMEM((HEADS, 2, HALF, 2 * HD), BF16),
            pltpu.VMEM((2, 2, GROUP, HALF, 2 * HD), BF16),
            pltpu.VMEM((2, 2, GROUP, HALF, 2 * HD), BF16),
            pltpu.VMEM((2, 2, SEG, 2 * HD), BF16),
            pltpu.VMEM((2, 2, HD, SEG), BF16),
            pltpu.VMEM((nz, 2, w_rows, width), BF16),
            pltpu.VMEM((3, KC, QB), F32),
            pltpu.VMEM((3, KC, QB), F32),
            pltpu.VMEM((2, 3, KC, 2 * QB), BF16),
            pltpu.VMEM((2, 2, SEG, 2 * HD), F32),
            pltpu.VMEM((KC, 2 * HD), F32),
            pltpu.VMEM((2, GROUP, 3, HALF, 2 * HD), BF16),
            pltpu.VMEM((HEADS, 3, HALF, 2 * HD), BF16),
            pltpu.VMEM((ROWS, width), BF16),
            dma((nz,)), dma((nz,)), dma((nz,)), dma((nz,)),
            dma((2, 2, GROUP)), dma((2, 2, GROUP)),
            dma((2,)), dma((2,)), dma((1,)), dma((1,)),
            dma((2, GROUP)), dma((2, GROUP)), dma((7,)),
        ],
        compiler_params=pltpu.CompilerParams(
            collective_id=0, has_side_effects=True, vmem_limit_bytes=56 * 1024 * 1024
        ),
        cost_estimate=pl.CostEstimate(flops=4_000_000_000, bytes_accessed=3_000_000, transcendentals=4_000_000),
    )(
        query_in[0], key_in[0], value_in[0], out_grad[0],
        w_out.reshape(2, w_rows, width), head_offsets, valid_tiles,
    )
    return tuple(o[None] for o in outs)


def solution(mesh):
    rows = P("fsdp", "ctx", None)
    return jax.shard_map(
        on_device,
        mesh=mesh,
        in_specs=(rows, rows, rows, rows, P("fsdp", None), P(), P("fsdp")),
        out_specs=(rows, rows, rows),
        check_vma=False,
    )
```

```python
import jax
import jax.numpy as jnp
from jax import lax
from jax.experimental import pallas as pl
from jax.experimental.pallas import tpu as pltpu
from jax.sharding import PartitionSpec as P

HEADS = 12
HD = 64
GROUP = 8
ROWS = 256
HALF = 128
QUAD = GROUP // 2
SEG = GROUP * HALF
QB = 256
KC = 512
SUB = 256
NEG = -1e30
PAIRS = 3
EARLY = 2
W_CUT = 32
BLOCKS = 6
F32 = jnp.float32
BF16 = jnp.bfloat16
MESH = pl.DeviceIdType.MESH


def nt(a, b):
    return lax.dot_general(a, b, (((1,), (1,)), ((), ())), preferred_element_type=F32)


def nn(a, b):
    return jnp.dot(a, b, preferred_element_type=F32)


def row_perm(value):
    r = lax.broadcasted_iota(jnp.int32, (ROWS, ROWS), 0)
    c = lax.broadcasted_iota(jnp.int32, (ROWS, ROWS), 1)
    pos = jnp.where(r < HALF, 2 * r, 2 * r - (ROWS - 1))
    return jnp.where(c == pos, value, 0.0).astype(BF16)


def row_unperm():
    r = lax.broadcasted_iota(jnp.int32, (ROWS, ROWS), 1)
    c = lax.broadcasted_iota(jnp.int32, (ROWS, ROWS), 0)
    pos = jnp.where(r < HALF, 2 * r, 2 * r - (ROWS - 1))
    return jnp.where(c == pos, 1.0, 0.0).astype(BF16)


def kernel(
    q_in, k_in, v_in, og_in, w_ref, off_ref, valid_ref,
    back,
    xin, qks, vs, gs, qk, vin, gin, vd, kp, kt, w4, ebuf, stat, dpbuf, dsp, acc, xsib, out, dqbuf, og_perm,
    w_send, w_recv, a_send, a_recv, f_send, f_recv, x_send, x_recv, o_send, o_recv,
    l_sem, in_sem,
):
    ctx = lax.axis_index("ctx")
    z = lax.axis_index("fsdp")
    nz = lax.axis_size("fsdp")
    m = ctx % GROUP
    base = ctx - m
    chip = m // 2
    core = m % 2
    half = m // QUAD
    valid = valid_ref[0]

    def dev(member):
        return (base + member, z)

    def remote(src, dst, ssem, rsem, to):
        return pltpu.make_async_remote_copy(
            src_ref=src, dst_ref=dst, send_sem=ssem, recv_sem=rsem, device_id=to, device_id_type=MESH
        )

    def full_head(p):
        return 3 * (p // 2) + 2 * (p % 2)

    barrier = pltpu.get_barrier_semaphore()
    for d in range(1, GROUP):
        pl.semaphore_signal(barrier, inc=1, device_id=dev(m ^ d), device_id_type=MESH)
    for d in (1, 2, nz - 2, nz - 1):
        pl.semaphore_signal(barrier, inc=1, device_id=(ctx, (z + d) % nz), device_id_type=MESH)
    loads = [pltpu.make_async_copy(x, xin.at[n], in_sem.at[n]) for n, x in enumerate((q_in, k_in, v_in, og_in))]
    for c in loads:
        c.start()
    own_w = pltpu.make_async_copy(w_ref, w4.at[z], l_sem.at[0])
    own_w.start()

    turn = 1 - 2 * core
    pieces = (pl.ds(0, W_CUT), pl.ds(W_CUT, w_ref.shape[1] - W_CUT))

    def w_copy(way, step, n, sender):
        by = turn if way == 0 else -turn
        hop = 2 if step == 4 else 1
        frm = (z - (step - hop if sender else step) * by + nz) % nz
        rows = pieces[n]
        src = w_ref.at[core, rows] if step == 1 else w4.at[frm, core, rows]
        return frm, remote(
            src, w4.at[frm, core, rows], w_send.at[0],
            w_recv.at[(way * 4 + step - 1) * 2 + n], (ctx, (z + hop * by + nz) % nz),
        )

    def arrived(ref, sem):
        pltpu.make_async_copy(ref, ref, sem).wait()

    def w_forward(frm, c):
        return remote(w4.at[frm, c], w4.at[frm, c], w_send.at[1], w_recv.at[16], dev(m ^ 1))

    lane = lax.broadcasted_iota(jnp.int32, (HALF, 2 * HD), 1)
    low = lane < HD

    def takes_odd(tile):
        return jnp.where(low, off_ref[1, 2 * tile], off_ref[1, 2 * tile + 1]) == 1

    def classes(x, odd):
        return jnp.where(odd, x[HALF:], x[:HALF]), jnp.where(odd, x[:HALF], x[HALF:])

    def side_by_side(l, r):
        one = jnp.where(low, l, pltpu.roll(r, HD, 1)).astype(BF16)
        return one, jnp.where(low, pltpu.roll(l, HD, 1), r).astype(BF16)

    def pack_pair(dst, left, right, tile):
        odd = takes_odd(tile)
        for cls, (l, r) in enumerate(zip(classes(left, odd), classes(right, odd))):
            dst[2 * tile, cls], dst[2 * tile + 1, cls] = side_by_side(l, r)

    def pack_one(dst, x, tile):
        dst[2 * tile], dst[2 * tile + 1] = side_by_side(*classes(x, takes_odd(tile)))

    def place(dst, slot, s):
        return dst.at[slot, :, s] if len(dst.shape) == 5 else dst.at[slot, s]

    def full_copy(src, dst, which, d):
        p = m ^ d
        return remote(
            src.at[full_head(p)], place(dst, 0, m), a_send.at[which], a_recv.at[which, 0], dev(p)
        )

    def shared_copy(src, dst, which, dx):
        to = chip ^ dx
        return remote(
            src.at[3 * to + 1], place(dst, 1, m), a_send.at[which], a_recv.at[which, 1],
            dev(2 * to + half),
        )

    def local_full(src, dst, which):
        return pltpu.make_async_copy(src.at[full_head(m)], place(dst, 0, m), a_recv.at[which, 0])

    def local_shared(src, dst, which):
        return pltpu.make_async_copy(src.at[3 * chip + 1], place(dst, 1, m), a_recv.at[which, 1])

    def exchange(src, dst, which):
        for d in range(1, GROUP):
            full_copy(src, dst, which, d).start()
        local_full(src, dst, which).start()
        for dx in range(1, QUAD):
            shared_copy(src, dst, which, dx).start()

        @pl.when(core != half)
        def _():
            shared_copy(src, dst, which, 0).start()

        @pl.when(core == half)
        def _():
            local_shared(src, dst, which).start()

    def wait_full(dst, which):
        arrived(dst.at[0], a_recv.at[which, 0])

    def wait_shared(dst, which):
        part = pl.ds(QUAD * core, QUAD)
        arrived(dst.at[1, :, part] if which == 0 else dst.at[1, part], a_recv.at[which, 1])

    def positions(row, cls, off):
        return base * ROWS + 2 * row + (off if cls == 0 else 1 - off)

    wide = lax.broadcasted_iota(jnp.int32, (KC, 2 * HD), 1)
    key_row = lax.broadcasted_iota(jnp.int32, (KC, 1), 0)

    def prepare(slot, cls, seg, off):
        bias = jnp.where(positions(seg * KC + key_row, cls, off) < valid, 0.0, NEG)
        x = qk[slot, cls, pl.ds(seg * QUAD, QUAD)].reshape(KC, 2 * HD).astype(F32)
        rows = pl.ds(pl.multiple_of(seg * KC, KC), KC)
        kp[slot, cls, rows] = jnp.where(wide >= HD, x, jnp.where(wide == 0, bias, 0.0)).astype(BF16)
        kt[slot, cls, :, rows] = jnp.transpose(x)[HD:].astype(BF16)

    def join(slot, cls, seg, with_grad):
        part = pl.ds(seg * QUAD, QUAD)
        x = vin[slot, part].reshape(KC, 2 * HD).astype(F32)
        g = 0.0
        if cls:
            x = pltpu.roll(x, HD, 1)
        if with_grad:
            g = gin[slot, part].reshape(KC, 2 * HD).astype(F32)
            if not cls:
                g = pltpu.roll(g, HD, 1)
        vd[slot, cls, part] = jnp.where(wide < HD, x, g).astype(BF16).reshape(QUAD, HALF, 2 * HD)

    qlane = lax.broadcasted_iota(jnp.int32, (QB, 2 * HD), 1)
    qlow = qlane < HD
    qrow = lax.broadcasted_iota(jnp.int32, (QB, 1), 0)

    def fold(x, op):
        return op(x.reshape(SUB // 8, 8, QB), axis=0)

    def chunks_of(c, cls):
        if cls == 0:
            return [(0, 0, c, 2), (1, 0, 1 - c, 1), (2, 1, c, 1)]
        return [(3, 0, c, 1), (4, 1, c, 1)]

    def scores(slot, off, c, i, cls):
        b = 4 * slot + (2 * c + i if slot == 0 else i)
        r0 = pl.multiple_of(c * KC + i * QB, QB)
        xq = qk[slot, cls, pl.ds(c * QUAD + 2 * i, 2)].reshape(QB, 2 * HD).astype(F32)
        use = jnp.where(positions(r0 + qrow, cls, off) < valid, 1.0, 0.0)
        qp = jnp.where(qlow, jnp.where(qlane == 0, use, 0.0), pltpu.roll(xq, HD, 1)).astype(BF16)
        chunks = chunks_of(c, cls)
        top = jnp.full((8, QB), -jnp.inf, F32)
        for n, kc, seg, mult in chunks:
            for u in range(KC // SUB):
                s = nt(kp[slot, kc, pl.ds(pl.multiple_of(seg * KC + u * SUB, SUB), SUB)], qp)
                ebuf[b, n, u * SUB:(u + 1) * SUB] = s
                top = jnp.maximum(top, fold(s, jnp.max))
        top = jnp.max(top, axis=0, keepdims=True)
        total = jnp.zeros((8, QB), F32)
        for n, kc, seg, mult in chunks:
            for u in range(KC // SUB):
                su = slice(u * SUB, (u + 1) * SUB)
                e = jnp.exp(ebuf[b, n, su] - top)
                ebuf[b, n, su] = e
                total = total + mult * fold(e, jnp.sum)
        stat[b, cls] = 1.0 / jnp.sum(total, axis=0, keepdims=True)

    def gradients(slot, c, i, cls):
        b = 4 * slot + (2 * c + i if slot == 0 else i)
        s0 = c * QUAD + 2 * i
        xq = qk[slot, cls, pl.ds(s0, 2)].reshape(QB, 2 * HD).astype(F32)
        xv = vd[slot, cls, pl.ds(s0, 2)].reshape(QB, 2 * HD).astype(F32)
        gp = jnp.where(qlow, 0.0, xv)
        g0 = gp.astype(BF16)
        gp = pltpu.roll(gp, HD, 1).astype(BF16)
        q0 = jnp.where(qlow, xq, 0.0).astype(BF16)
        grads = jnp.concatenate([q0, g0], axis=0)
        chunks = chunks_of(c, cls)
        dot_sum = jnp.zeros((8, QB), F32)
        for n, kc, seg, mult in chunks:
            for u in range(KC // SUB):
                su = slice(u * SUB, (u + 1) * SUB)
                per = SUB // HALF
                values = vd[slot, kc, pl.ds(seg * QUAD + u * per, per)].reshape(SUB, 2 * HD)
                dp = nt(values, gp)
                dpbuf[n, su] = dp
                dot_sum = dot_sum + mult * fold(ebuf[b, n, su] * dp, jnp.sum)
        inv = stat[b, cls]
        delta = jnp.sum(dot_sum, axis=0, keepdims=True) * inv
        dqt = jnp.zeros((HD, QB), F32)
        for n, kc, seg, mult in chunks:
            rows = pl.ds(pl.multiple_of(seg * KC, KC), KC)
            for u in range(KC // SUB):
                su = slice(u * SUB, (u + 1) * SUB)
                p = ebuf[b, n, su] * inv
                ds = p * (dpbuf[n, su] - delta)
                dsp[n, su, :QB] = ds.astype(BF16)
                dsp[n, su, QB:] = p.astype(BF16)
            acc[slot, kc, rows] += nn(dsp[n], grads * mult if mult != 1 else grads)
            keys_t = kt[slot, kc, :, rows]
            dqt = dqt + nn(keys_t * mult if mult != 1 else keys_t, dsp[n, :, :QB])
        return dqt

    def put_dq(slot, s0, sel, oth):
        dq = jnp.transpose(jnp.concatenate([sel, oth], axis=0)) * (HD ** -0.5)
        out[slot, pl.ds(s0, 2), 2] = dq.reshape(2, HALF, 2 * HD).astype(BF16)

    def send_out(slot, s, kind):
        head = full_head(m) if slot == 0 else 3 * chip + 1
        return remote(
            out.at[slot, s, kind], back.at[head, kind], o_send.at[0], o_recv.at[0], dev(s)
        )

    def keep_out(slot, kind):
        head = full_head(m) if slot == 0 else 3 * chip + 1
        return pltpu.make_async_copy(out.at[slot, m, kind], back.at[head, kind], o_recv.at[0])

    def start_out(slot, s, kind):
        @pl.when(s != m)
        def _():
            send_out(slot, s, kind).start()

        @pl.when(s == m)
        def _():
            keep_out(slot, kind).start()

    mine = pl.ds(QUAD * core, QUAD)
    theirs = pl.ds(QUAD * (1 - core), QUAD)

    def pass_on(dst, which, part):
        ref = dst.at[1, 0, part] if which == 0 else dst.at[1, part]
        return remote(ref, ref, f_send.at[which], f_recv.at[which], dev(m ^ 1))

    off0 = off_ref[1, full_head(m)]
    off1 = off_ref[1, 3 * chip + 1]

    perm = row_perm(1.0)
    perm_q = row_perm(HD ** -0.5)
    loads[0].wait()
    loads[1].wait()
    for t in range(HEADS // 2):
        cols = slice(t * 128, (t + 1) * 128)
        pack_pair(qks, nn(perm_q, xin[0, :, cols]), nn(perm, xin[1, :, cols]), t)
    pl.semaphore_wait(barrier, GROUP - 1 + 4)
    for n in range(2):
        for way in range(2):
            w_copy(way, 1, n, True)[1].start()
    exchange(qks, qk, 0)

    loads[2].wait()
    for t in range(HEADS // 2):
        pack_one(vs, nn(perm, xin[2, :, t * 128:(t + 1) * 128]), t)
    exchange(vs, vin, 1)

    loads[3].wait()
    og_perm[...] = nn(perm, xin[3]).astype(BF16)
    acc[...] = jnp.zeros_like(acc)
    for step in range(1, 4):
        for n in range(2):
            for way in range(2):
                frm, arrival = w_copy(way, step, n, False)
                arrival.wait_recv()
                if step < 3:
                    w_copy(way, step + 1, n, True)[1].start()
                if step == 2 and n == way:
                    w_copy(way, 4, n, True)[1].start()
                if n == 1:
                    w_forward(frm, core).start()

    wait_full(qk, 0)
    for cls in range(2):
        for seg in range(2):
            prepare(0, cls, seg, off0)

    @pl.loop(0, EARLY)
    def _(t):
        for cls in range(2):
            scores(0, off0, t // 2, t % 2, cls)

    for way in range(2):
        frm, arrival = w_copy(way, 4, way, False)
        arrival.wait_recv()
    w_forward(frm, core).start()
    own_w.wait()
    arrived(w4.at[pl.ds(0, nz - 1), 0], w_recv.at[16])
    grad = nt(og_perm[...], w4[...].reshape(HEADS * HD, HEADS * HD))
    r = lax.broadcasted_iota(jnp.int32, (ROWS, 1), 0)
    position = ctx * ROWS + jnp.where(r < HALF, 2 * r, 2 * r - (ROWS - 1))
    grad = jnp.where(position < valid, grad, 0.0)
    for t in range(HEADS // 2):
        cols = slice(t * 128, (t + 1) * 128)
        pack_one(gs, grad[:, cols], t)
    exchange(gs, gin, 2)

    wait_shared(qk, 0)
    pass_on(qk, 0, mine).start()

    @pl.loop(EARLY, 4)
    def _(t):
        for cls in range(2):
            scores(0, off0, t // 2, t % 2, cls)

    pass_on(qk, 0, theirs).wait_recv()
    prepare(1, 0, 0, off1)
    prepare(1, 0, 1, off1)
    prepare(1, 1, core, off1)

    @pl.loop(0, 2)
    def _(t):
        for cls in range(2):
            scores(1, off1, core, t, cls)

    def segment(slot, c, middle):
        @pl.loop(0, 2)
        def _(i):
            dqbuf[i] = gradients(slot, c, i, 0)

        middle()

        @pl.loop(0, 2)
        def _(i):
            s0 = QUAD * c + 2 * i
            put_dq(slot, s0, dqbuf[i], gradients(slot, c, i, 1))
            for e in range(2):
                start_out(slot, s0 + e, 2)

    def send_terms(slot, cls, c, extra=None):
        x = acc[slot, cls, pl.ds(pl.multiple_of(c * KC, KC), KC)]
        if extra is not None:
            x = x + extra
        out[slot, pl.ds(QUAD * c, QUAD), cls] = x.reshape(QUAD, HALF, 2 * HD).astype(BF16)
        for j in range(QUAD):
            start_out(slot, QUAD * c + j, cls)

    def swap_terms(c):
        rows = pl.ds(pl.multiple_of(c * KC, KC), KC)
        return remote(acc.at[1, 0, rows], xsib, x_send.at[0], x_recv.at[0], dev(m ^ 1))

    wait_shared(vin, 1)
    pass_on(vin, 1, mine).start()
    wait_shared(gin, 2)
    join(1, 0, core, True)
    join(1, 1, core, True)
    pass_on(vin, 1, theirs).wait_recv()
    join(1, 0, 1 - core, False)
    segment(1, core, lambda: swap_terms(1 - core).start())
    send_terms(1, 1, core)
    swap_terms(core).wait_recv()
    send_terms(1, 0, core, xsib[...])

    wait_full(vin, 1)
    wait_full(gin, 2)
    for cls in range(2):
        for c in range(2):
            join(0, cls, c, True)
    segment(0, core, lambda: None)
    send_terms(0, 1, core)
    segment(0, 1 - core, lambda: send_terms(0, 0, core))
    send_terms(0, 1, 1 - core)
    send_terms(0, 0, 1 - core)

    arrived(back, o_recv.at[0])

    arrived(w4.at[pl.ds(0, nz - 1), 0], w_send.at[0])
    arrived(w4.at[pl.ds(0, nz - 1), 0], w_send.at[1])
    swap_terms(1 - core).wait_send()
    pass_on(qk, 0, mine).wait_send()
    pass_on(vin, 1, mine).wait_send()

    def all_left(blocks):
        for which, src in enumerate((qks, vs, gs)):
            arrived(src.at[pl.ds(0, blocks)], a_send.at[which])
        arrived(back.at[pl.ds(0, blocks)], o_send.at[0])

    @pl.when(core != half)
    def _():
        all_left(GROUP - 1 + QUAD)

    @pl.when(core == half)
    def _():
        all_left(GROUP - 1 + QUAD - 1)


def finish(off_ref, back, dq_ref, dk_ref, dv_ref):
    lane = lax.broadcasted_iota(jnp.int32, (HALF, 2 * HD), 1)
    low = lane < HD
    unperm = row_unperm()
    first = pl.program_id(0) * PAIRS
    for t in range(PAIRS):
        cols = slice(t * 128, (t + 1) * 128)
        odd = jnp.where(low, off_ref[1, 2 * (first + t)], off_ref[1, 2 * (first + t) + 1]) == 1

        def put(ref, sel, oth):
            rows = jnp.concatenate([jnp.where(odd, oth, sel), jnp.where(odd, sel, oth)], axis=0)
            ref[:, cols] = nn(unperm, rows.astype(BF16)).astype(BF16)

        one = [back[2 * t, n].astype(F32) for n in range(3)]
        two = [back[2 * t + 1, n].astype(F32) for n in range(3)]
        left = [jnp.where(low, one[n], pltpu.roll(two[n], HD, 1)) for n in range(3)]
        right = [jnp.where(low, pltpu.roll(one[n], HD, 1), two[n]) for n in range(3)]
        put(dk_ref, left[0], left[1])
        put(dv_ref, right[0], right[1])
        put(dq_ref, left[2], right[2])


def on_device(query_in, key_in, value_in, out_grad, w_out, head_offsets, valid_tiles):
    width = HEADS * HD
    nz = lax.axis_size("fsdp")
    w_rows = w_out.shape[0] // 2
    far = pl.BlockSpec(memory_space=pl.ANY)
    smem = pl.BlockSpec(memory_space=pltpu.SMEM)
    dma = pltpu.SemaphoreType.DMA
    back = pl.pallas_call(
        kernel,
        out_shape=jax.ShapeDtypeStruct((HEADS, 3, HALF, 2 * HD), BF16),
        in_specs=[far] * 5 + [smem] * 2,
        out_specs=far,
        scratch_shapes=[
            pltpu.VMEM((4, ROWS, width), BF16),
            pltpu.VMEM((HEADS, 2, HALF, 2 * HD), BF16),
            pltpu.VMEM((HEADS, HALF, 2 * HD), BF16),
            pltpu.VMEM((HEADS, HALF, 2 * HD), BF16),
            pltpu.VMEM((2, 2, GROUP, HALF, 2 * HD), BF16),
            pltpu.VMEM((2, GROUP, HALF, 2 * HD), BF16),
            pltpu.VMEM((2, GROUP, HALF, 2 * HD), BF16),
            pltpu.VMEM((2, 2, GROUP, HALF, 2 * HD), BF16),
            pltpu.VMEM((2, 2, SEG, 2 * HD), BF16),
            pltpu.VMEM((2, 2, HD, SEG), BF16),
            pltpu.VMEM((nz, 2, w_rows, width), BF16),
            pltpu.VMEM((BLOCKS, 5, KC, QB), F32),
            pltpu.VMEM((BLOCKS, 2, 1, QB), F32),
            pltpu.VMEM((5, KC, QB), F32),
            pltpu.VMEM((5, KC, 2 * QB), BF16),
            pltpu.VMEM((2, 2, SEG, 2 * HD), F32),
            pltpu.VMEM((KC, 2 * HD), F32),
            pltpu.VMEM((2, GROUP, 3, HALF, 2 * HD), BF16),
            pltpu.VMEM((2, HD, QB), F32),
            pltpu.VMEM((ROWS, width), BF16),
            dma((2,)), dma((17,)), dma((3,)), dma((3, 2)),
            dma((2,)), dma((2,)), dma((1,)), dma((1,)), dma((1,)), dma((1,)), dma((1,)), dma((4,)),
        ],
        compiler_params=pltpu.CompilerParams(
            collective_id=0, has_side_effects=True, vmem_limit_bytes=56 * 1024 * 1024
        ),
        cost_estimate=pl.CostEstimate(flops=4_000_000_000, bytes_accessed=3_000_000, transcendentals=4_000_000),
    )(
        query_in[0], key_in[0], value_in[0], out_grad[0],
        w_out.reshape(2, w_rows, width), head_offsets, valid_tiles,
    )
    columns = pl.BlockSpec((ROWS, PAIRS * 2 * HD), lambda t: (0, t))
    outs = pl.pallas_call(
        finish,
        grid=(HEADS // 2 // PAIRS,),
        out_shape=[jax.ShapeDtypeStruct((ROWS, width), BF16)] * 3,
        in_specs=[smem, pl.BlockSpec((2 * PAIRS, 3, HALF, 2 * HD), lambda t: (t, 0, 0, 0))],
        out_specs=[columns] * 3,
    )(head_offsets, back)
    return tuple(o[None] for o in outs)


def solution(mesh):
    rows = P("fsdp", "ctx", None)
    return jax.shard_map(
        on_device,
        mesh=mesh,
        in_specs=(rows, rows, rows, rows, P("fsdp", None), P(), P("fsdp")),
        out_specs=(rows, rows, rows),
        check_vma=False,
    )
```

```python
import jax
import jax.numpy as jnp
from jax import lax
from jax.experimental import pallas as pl
from jax.experimental.pallas import tpu as pltpu
from jax.sharding import PartitionSpec as P

HEADS = 12
HD = 64
GROUP = 8
ROWS = 256
HALF = 128
QUAD = GROUP // 2
SEG = GROUP * HALF
QB = 256
KC = 512
SUB = 256
NEG = -1e30
PAIRS = 3
EARLY = 2
W_CUT = 32
BLOCKS = 6
F32 = jnp.float32
BF16 = jnp.bfloat16
MESH = pl.DeviceIdType.MESH


def nt(a, b):
    return lax.dot_general(a, b, (((1,), (1,)), ((), ())), preferred_element_type=F32)


def nn(a, b):
    return jnp.dot(a, b, preferred_element_type=F32)


def row_perm(value):
    r = lax.broadcasted_iota(jnp.int32, (ROWS, ROWS), 0)
    c = lax.broadcasted_iota(jnp.int32, (ROWS, ROWS), 1)
    pos = jnp.where(r < HALF, 2 * r, 2 * r - (ROWS - 1))
    return jnp.where(c == pos, value, 0.0).astype(BF16)


def row_unperm():
    r = lax.broadcasted_iota(jnp.int32, (ROWS, ROWS), 1)
    c = lax.broadcasted_iota(jnp.int32, (ROWS, ROWS), 0)
    pos = jnp.where(r < HALF, 2 * r, 2 * r - (ROWS - 1))
    return jnp.where(c == pos, 1.0, 0.0).astype(BF16)


def kernel(
    q_in, k_in, v_in, og_in, w_ref, off_ref, valid_ref,
    back,
    xin, qks, vs, gs, qk, vin, gin, vd, kp, kt, w4, ebuf, stat, dpbuf, dsp, acc, xsib, out, og_perm,
    w_send, w_recv, a_send, a_recv, f_send, f_recv, x_send, x_recv, o_send, o_recv,
    l_sem, in_sem,
):
    ctx = lax.axis_index("ctx")
    z = lax.axis_index("fsdp")
    nz = lax.axis_size("fsdp")
    m = ctx % GROUP
    base = ctx - m
    chip = m // 2
    core = m % 2
    half = m // QUAD
    valid = valid_ref[0]

    def dev(member):
        return (base + member, z)

    def remote(src, dst, ssem, rsem, to):
        return pltpu.make_async_remote_copy(
            src_ref=src, dst_ref=dst, send_sem=ssem, recv_sem=rsem, device_id=to, device_id_type=MESH
        )

    def full_head(p):
        return 3 * (p // 2) + 2 * (p % 2)

    barrier = pltpu.get_barrier_semaphore()
    for d in range(1, GROUP):
        pl.semaphore_signal(barrier, inc=1, device_id=dev(m ^ d), device_id_type=MESH)
    for d in (1, 2, nz - 2, nz - 1):
        pl.semaphore_signal(barrier, inc=1, device_id=(ctx, (z + d) % nz), device_id_type=MESH)
    loads = [pltpu.make_async_copy(x, xin.at[n], in_sem.at[n]) for n, x in enumerate((q_in, k_in, v_in, og_in))]
    for c in loads:
        c.start()
    own_w = pltpu.make_async_copy(w_ref, w4.at[z], l_sem.at[0])
    own_w.start()

    turn = 1 - 2 * core
    pieces = (pl.ds(0, W_CUT), pl.ds(W_CUT, w_ref.shape[1] - W_CUT))

    def w_copy(way, step, n, sender):
        by = turn if way == 0 else -turn
        hop = 2 if step == 4 else 1
        frm = (z - (step - hop if sender else step) * by + nz) % nz
        rows = pieces[n]
        src = w_ref.at[core, rows] if step == 1 else w4.at[frm, core, rows]
        return frm, remote(
            src, w4.at[frm, core, rows], w_send.at[0],
            w_recv.at[(way * 4 + step - 1) * 2 + n], (ctx, (z + hop * by + nz) % nz),
        )

    def arrived(ref, sem):
        pltpu.make_async_copy(ref, ref, sem).wait()

    def w_forward(frm, c):
        return remote(w4.at[frm, c], w4.at[frm, c], w_send.at[1], w_recv.at[16], dev(m ^ 1))

    lane = lax.broadcasted_iota(jnp.int32, (HALF, 2 * HD), 1)
    low = lane < HD

    def takes_odd(tile):
        return jnp.where(low, off_ref[1, 2 * tile], off_ref[1, 2 * tile + 1]) == 1

    def classes(x, odd):
        return jnp.where(odd, x[HALF:], x[:HALF]), jnp.where(odd, x[:HALF], x[HALF:])

    def side_by_side(l, r):
        one = jnp.where(low, l, pltpu.roll(r, HD, 1)).astype(BF16)
        return one, jnp.where(low, pltpu.roll(l, HD, 1), r).astype(BF16)

    def pack_pair(dst, left, right, tile):
        odd = takes_odd(tile)
        for cls, (l, r) in enumerate(zip(classes(left, odd), classes(right, odd))):
            dst[2 * tile, cls], dst[2 * tile + 1, cls] = side_by_side(l, r)

    def pack_one(dst, x, tile):
        dst[2 * tile], dst[2 * tile + 1] = side_by_side(*classes(x, takes_odd(tile)))

    def place(dst, slot, s, to_core):
        s = s ^ (QUAD * to_core)
        return dst.at[slot, :, s] if len(dst.shape) == 5 else dst.at[slot, s]

    def full_copy(src, dst, which, d):
        p = m ^ d
        return remote(
            src.at[full_head(p)], place(dst, 0, m, p % 2), a_send.at[which], a_recv.at[which, 0], dev(p)
        )

    def shared_copy(src, dst, which, dx):
        to = chip ^ dx
        return remote(
            src.at[3 * to + 1], place(dst, 1, m, half), a_send.at[which], a_recv.at[which, 1],
            dev(2 * to + half),
        )

    def local_full(src, dst, which):
        return pltpu.make_async_copy(src.at[full_head(m)], place(dst, 0, m, core), a_recv.at[which, 0])

    def local_shared(src, dst, which):
        return pltpu.make_async_copy(src.at[3 * chip + 1], place(dst, 1, m, half), a_recv.at[which, 1])

    def exchange(src, dst, which, shared_first=False):
        def send_full():
            for d in range(1, GROUP):
                full_copy(src, dst, which, d).start()
            local_full(src, dst, which).start()

        if not shared_first:
            send_full()
        for dx in range(1, QUAD):
            shared_copy(src, dst, which, dx).start()

        @pl.when(core != half)
        def _():
            shared_copy(src, dst, which, 0).start()

        @pl.when(core == half)
        def _():
            local_shared(src, dst, which).start()

        if shared_first:
            send_full()

    def wait_full(dst, which):
        arrived(dst.at[0], a_recv.at[which, 0])

    def wait_shared(dst, which):
        arrived(dst.at[1, :, 0:QUAD] if which == 0 else dst.at[1, 0:QUAD], a_recv.at[which, 1])

    def positions(row, cls, off):
        return base * ROWS + 2 * row + (off if cls == 0 else 1 - off)

    wide = lax.broadcasted_iota(jnp.int32, (KC, 2 * HD), 1)
    key_row = lax.broadcasted_iota(jnp.int32, (KC, 1), 0)

    def prepare(slot, cls, seg, off):
        bias = jnp.where(positions((seg ^ core) * KC + key_row, cls, off) < valid, 0.0, NEG)
        x = qk[slot, cls, seg * QUAD:(seg + 1) * QUAD].reshape(KC, 2 * HD).astype(F32)
        rows = slice(seg * KC, (seg + 1) * KC)
        kp[slot, cls, rows] = jnp.where(wide >= HD, x, jnp.where(wide == 0, bias, 0.0)).astype(BF16)
        kt[slot, cls, :, rows] = jnp.transpose(x)[HD:].astype(BF16)

    def join(slot, cls, seg, with_grad):
        part = slice(seg * QUAD, (seg + 1) * QUAD)
        x = vin[slot, part].reshape(KC, 2 * HD).astype(F32)
        g = 0.0
        if cls:
            x = pltpu.roll(x, HD, 1)
        if with_grad:
            g = gin[slot, part].reshape(KC, 2 * HD).astype(F32)
            if not cls:
                g = pltpu.roll(g, HD, 1)
        vd[slot, cls, part] = jnp.where(wide < HD, x, g).astype(BF16).reshape(QUAD, HALF, 2 * HD)

    qlane = lax.broadcasted_iota(jnp.int32, (QB, 2 * HD), 1)
    qlow = qlane < HD
    qrow = lax.broadcasted_iota(jnp.int32, (QB, 1), 0)

    def fold(x, op):
        return op(x.reshape(SUB // 8, 8, QB), axis=0)

    def chunks_of(c, cls):
        if cls == 0:
            return [(0, 0, c, 2), (1, 0, 1 - c, 1), (2, 1, c, 1)]
        return [(3, 0, c, 1), (4, 1, c, 1)]

    def scores(slot, off, c, i, cls):
        b = 4 * slot + 2 * c + i
        r0 = (c ^ core) * KC + i * QB
        xq = qk[slot, cls, c * QUAD + 2 * i:c * QUAD + 2 * i + 2].reshape(QB, 2 * HD).astype(F32)
        use = jnp.where(positions(r0 + qrow, cls, off) < valid, 1.0, 0.0)
        qp = jnp.where(qlow, jnp.where(qlane == 0, use, 0.0), pltpu.roll(xq, HD, 1)).astype(BF16)
        chunks = chunks_of(c, cls)
        top = jnp.full((8, QB), -jnp.inf, F32)
        for n, kc, seg, mult in chunks:
            for u in range(KC // SUB):
                s = nt(kp[slot, kc, seg * KC + u * SUB:seg * KC + (u + 1) * SUB], qp)
                ebuf[b, n, u * SUB:(u + 1) * SUB] = s
                top = jnp.maximum(top, fold(s, jnp.max))
        top = jnp.max(top, axis=0, keepdims=True)
        total = jnp.zeros((8, QB), F32)
        for n, kc, seg, mult in chunks:
            for u in range(KC // SUB):
                su = slice(u * SUB, (u + 1) * SUB)
                e = jnp.exp(ebuf[b, n, su] - top)
                ebuf[b, n, su] = e
                total = total + mult * fold(e, jnp.sum)
        stat[b, cls] = 1.0 / jnp.sum(total, axis=0, keepdims=True)

    def send_out(slot, c, j, kind):
        j = j ^ (m % QUAD)
        head = full_head(m) if slot == 0 else 3 * chip + 1
        return remote(
            out.at[slot, QUAD * c + j, kind], back.at[head, kind], o_send.at[0], o_recv.at[0],
            dev(QUAD * (c ^ core) + j),
        )

    def start_others(slot, c, kind):
        for j in range(1, QUAD):
            send_out(slot, c, j, kind).start()

    def start_last(slot, c, kinds):
        head = full_head(m) if slot == 0 else 3 * chip + 1

        @pl.when((c ^ core) != half)
        def _():
            for kind in kinds:
                send_out(slot, c, 0, kind).start()

        @pl.when((c ^ core) == half)
        def _():
            for kind in kinds:
                pltpu.make_async_copy(
                    out.at[slot, QUAD * c + m % QUAD, kind], back.at[head, kind], o_recv.at[0]
                ).start()

    def put_terms(slot, cls, c, x):
        out[slot, QUAD * c:QUAD * (c + 1), cls] = x.reshape(QUAD, HALF, 2 * HD).astype(BF16)
        start_others(slot, c, cls)

    def segment(slot, c, order, take):
        rows = {}
        stats = {}
        for cls in range(2):
            for i in range(2):
                b = 4 * slot + 2 * c + i
                s0 = c * QUAD + 2 * i
                xq = qk[slot, cls, s0:s0 + 2].reshape(QB, 2 * HD).astype(F32)
                xv = vd[slot, cls, s0:s0 + 2].reshape(QB, 2 * HD).astype(F32)
                g = jnp.where(qlow, 0.0, xv)
                rows[cls, i] = jnp.concatenate([jnp.where(qlow, xq, 0.0).astype(BF16), g.astype(BF16)], axis=0)
                gp = pltpu.roll(g, HD, 1).astype(BF16)
                dot_sum = jnp.zeros((8, QB), F32)
                for n, kc, seg, mult in chunks_of(c, cls):
                    for u in range(KC // SUB):
                        su = slice(u * SUB, (u + 1) * SUB)
                        per = SUB // HALF
                        s1 = seg * QUAD + u * per
                        dp = nt(vd[slot, kc, s1:s1 + per].reshape(SUB, 2 * HD), gp)
                        dpbuf[i, n, su] = dp
                        dot_sum = dot_sum + mult * fold(ebuf[b, n, su] * dp, jnp.sum)
                inv = stat[b, cls]
                stats[cls, i] = (inv, jnp.sum(dot_sum, axis=0, keepdims=True) * inv)
        dqt = {}
        for kc, seg in order:
            terms = None
            for cls in range(2):
                for n, kn, sn, mult in chunks_of(c, cls):
                    if (kn, sn) != (kc, seg):
                        continue
                    keys_t = kt[slot, kc, :, seg * KC:(seg + 1) * KC]
                    keys_t = keys_t * mult if mult != 1 else keys_t
                    for i in range(2):
                        b = 4 * slot + 2 * c + i
                        inv, delta = stats[cls, i]
                        for u in range(KC // SUB):
                            su = slice(u * SUB, (u + 1) * SUB)
                            p = ebuf[b, n, su] * inv
                            ds = p * (dpbuf[i, n, su] - delta)
                            dsp[i, n, su, :QB] = ds.astype(BF16)
                            dsp[i, n, su, QB:] = p.astype(BF16)
                        g = rows[cls, i] * mult if mult != 1 else rows[cls, i]
                        t = nn(dsp[i, n], g)
                        terms = t if terms is None else terms + t
                        t = nn(keys_t, dsp[i, n, :, :QB])
                        dqt[cls, i] = dqt[cls, i] + t if (cls, i) in dqt else t
            take(kc, seg, terms)
        for i in range(2):
            s0 = QUAD * c + 2 * i
            dq = jnp.transpose(jnp.concatenate([dqt[0, i], dqt[1, i]], axis=0)) * (HD ** -0.5)
            out[slot, s0:s0 + 2, 2] = dq.reshape(2, HALF, 2 * HD).astype(BF16)
        start_others(slot, c, 2)

    first, other = slice(0, QUAD), slice(QUAD, GROUP)

    def pass_on(dst, which):
        src, to = (dst.at[1, 0, first], dst.at[1, 0, other]) if which == 0 else (dst.at[1, first], dst.at[1, other])
        return remote(src, to, f_send.at[which], f_recv.at[which], dev(m ^ 1))

    off0 = off_ref[1, full_head(m)]
    off1 = off_ref[1, 3 * chip + 1]

    pl.semaphore_wait(barrier, GROUP - 1 + 4)
    for n in range(2):
        for way in range(2):
            w_copy(way, 1, n, True)[1].start()

    perm = row_perm(1.0)
    perm_q = row_perm(HD ** -0.5)
    loads[0].wait()
    loads[1].wait()
    for t in range(HEADS // 2):
        cols = slice(t * 128, (t + 1) * 128)
        pack_pair(qks, nn(perm_q, xin[0, :, cols]), nn(perm, xin[1, :, cols]), t)
    exchange(qks, qk, 0)

    loads[2].wait()
    for t in range(HEADS // 2):
        pack_one(vs, nn(perm, xin[2, :, t * 128:(t + 1) * 128]), t)
    exchange(vs, vin, 1)

    loads[3].wait()
    og_perm[...] = nn(perm, xin[3]).astype(BF16)
    for step in range(1, 4):
        for n in range(2):
            for way in range(2):
                frm, arrival = w_copy(way, step, n, False)
                arrival.wait_recv()
                if step < 3:
                    w_copy(way, step + 1, n, True)[1].start()
                if step == 2 and n == way:
                    w_copy(way, 4, n, True)[1].start()
                if n == 1:
                    w_forward(frm, core).start()

    wait_full(qk, 0)
    for cls in range(2):
        for seg in range(2):
            prepare(0, cls, seg, off0)

    for t in range(EARLY):
        for cls in range(2):
            scores(0, off0, t // 2, t % 2, cls)

    for way in range(2):
        frm, arrival = w_copy(way, 4, way, False)
        arrival.wait_recv()
    w_forward(frm, core).start()
    own_w.wait()
    arrived(w4.at[pl.ds(0, nz - 1), 0], w_recv.at[16])
    grad = nt(og_perm[...], w4[...].reshape(HEADS * HD, HEADS * HD))
    r = lax.broadcasted_iota(jnp.int32, (ROWS, 1), 0)
    position = ctx * ROWS + jnp.where(r < HALF, 2 * r, 2 * r - (ROWS - 1))
    grad = jnp.where(position < valid, grad, 0.0)
    for t in range(HEADS // 2):
        cols = slice(t * 128, (t + 1) * 128)
        pack_one(gs, grad[:, cols], t)
    exchange(gs, gin, 2, shared_first=True)

    wait_shared(qk, 0)
    pass_on(qk, 0).start()

    for t in range(EARLY, 4):
        for cls in range(2):
            scores(0, off0, t // 2, t % 2, cls)

    pass_on(qk, 0).wait_recv()
    prepare(1, 0, 0, off1)
    prepare(1, 0, 1, off1)
    prepare(1, 1, 0, off1)

    for t in range(2):
        for cls in range(2):
            scores(1, off1, 0, t, cls)

    swap_terms = remote(acc.at[0], xsib, x_send.at[0], x_recv.at[0], dev(m ^ 1))

    def take_shared(kc, seg, x):
        if kc:
            put_terms(1, 1, 0, x)
        elif seg:
            acc[0] = x
            swap_terms.start()
        else:
            swap_terms.wait_recv()
            put_terms(1, 0, 0, x + xsib[...])

    def take_first(kc, seg, x):
        if kc:
            put_terms(0, 1, 0, x)
        else:
            acc[1 + seg] = x

    def take_second(kc, seg, x):
        put_terms(0, kc, seg, x if kc else x + acc[1 + seg])

    wait_shared(vin, 1)
    pass_on(vin, 1).start()
    wait_shared(gin, 2)
    join(1, 0, 0, True)
    join(1, 1, 0, True)
    pass_on(vin, 1).wait_recv()
    join(1, 0, 1, False)
    segment(1, 0, ((0, 1), (1, 0), (0, 0)), take_shared)
    start_last(1, 0, (1, 0, 2))

    wait_full(vin, 1)
    wait_full(gin, 2)
    for cls in range(2):
        for c in range(2):
            join(0, cls, c, True)
    segment(0, 0, ((1, 0), (0, 0), (0, 1)), take_first)
    start_last(0, 0, (1, 2))
    segment(0, 1, ((0, 0), (0, 1), (1, 1)), take_second)
    start_last(0, 0, (0,))
    start_last(0, 1, (0, 1, 2))

    arrived(back, o_recv.at[0])

    arrived(w4.at[pl.ds(0, nz - 1), 0], w_send.at[0])
    arrived(w4.at[pl.ds(0, nz - 1), 0], w_send.at[1])
    swap_terms.wait_send()
    pass_on(qk, 0).wait_send()
    pass_on(vin, 1).wait_send()

    def all_left(blocks):
        for which, src in enumerate((qks, vs, gs)):
            arrived(src.at[pl.ds(0, blocks)], a_send.at[which])
        arrived(back.at[pl.ds(0, blocks)], o_send.at[0])

    @pl.when(core != half)
    def _():
        all_left(GROUP - 1 + QUAD)

    @pl.when(core == half)
    def _():
        all_left(GROUP - 1 + QUAD - 1)


def finish(off_ref, back, dq_ref, dk_ref, dv_ref):
    lane = lax.broadcasted_iota(jnp.int32, (HALF, 2 * HD), 1)
    low = lane < HD
    unperm = row_unperm()
    first = pl.program_id(0) * PAIRS
    for t in range(PAIRS):
        cols = slice(t * 128, (t + 1) * 128)
        odd = jnp.where(low, off_ref[1, 2 * (first + t)], off_ref[1, 2 * (first + t) + 1]) == 1

        def put(ref, sel, oth):
            rows = jnp.concatenate([jnp.where(odd, oth, sel), jnp.where(odd, sel, oth)], axis=0)
            ref[:, cols] = nn(unperm, rows.astype(BF16)).astype(BF16)

        one = [back[2 * (first + t), n].astype(F32) for n in range(3)]
        two = [back[2 * (first + t) + 1, n].astype(F32) for n in range(3)]
        left = [jnp.where(low, one[n], pltpu.roll(two[n], HD, 1)) for n in range(3)]
        right = [jnp.where(low, pltpu.roll(one[n], HD, 1), two[n]) for n in range(3)]
        put(dk_ref, left[0], left[1])
        put(dv_ref, right[0], right[1])
        put(dq_ref, left[2], right[2])


def on_device(query_in, key_in, value_in, out_grad, w_out, head_offsets, valid_tiles):
    width = HEADS * HD
    nz = lax.axis_size("fsdp")
    w_rows = w_out.shape[0] // 2
    far = pl.BlockSpec(memory_space=pl.ANY)
    smem = pl.BlockSpec(memory_space=pltpu.SMEM)
    dma = pltpu.SemaphoreType.DMA
    back = pl.pallas_call(
        kernel,
        out_shape=pltpu.VMEM((HEADS, 3, HALF, 2 * HD), BF16),
        in_specs=[far] * 5 + [smem] * 2,
        out_specs=pl.BlockSpec(memory_space=pltpu.VMEM),
        scratch_shapes=[
            pltpu.VMEM((4, ROWS, width), BF16),
            pltpu.VMEM((HEADS, 2, HALF, 2 * HD), BF16),
            pltpu.VMEM((HEADS, HALF, 2 * HD), BF16),
            pltpu.VMEM((HEADS, HALF, 2 * HD), BF16),
            pltpu.VMEM((2, 2, GROUP, HALF, 2 * HD), BF16),
            pltpu.VMEM((2, GROUP, HALF, 2 * HD), BF16),
            pltpu.VMEM((2, GROUP, HALF, 2 * HD), BF16),
            pltpu.VMEM((2, 2, GROUP, HALF, 2 * HD), BF16),
            pltpu.VMEM((2, 2, SEG, 2 * HD), BF16),
            pltpu.VMEM((2, 2, HD, SEG), BF16),
            pltpu.VMEM((nz, 2, w_rows, width), BF16),
            pltpu.VMEM((BLOCKS, 5, KC, QB), F32),
            pltpu.VMEM((BLOCKS, 2, 1, QB), F32),
            pltpu.VMEM((2, 5, KC, QB), F32),
            pltpu.VMEM((2, 5, KC, 2 * QB), BF16),
            pltpu.VMEM((3, KC, 2 * HD), F32),
            pltpu.VMEM((KC, 2 * HD), F32),
            pltpu.VMEM((2, GROUP, 3, HALF, 2 * HD), BF16),
            pltpu.VMEM((ROWS, width), BF16),
            dma((2,)), dma((17,)), dma((3,)), dma((3, 2)),
            dma((2,)), dma((2,)), dma((1,)), dma((1,)), dma((1,)), dma((1,)), dma((1,)), dma((4,)),
        ],
        compiler_params=pltpu.CompilerParams(
            collective_id=0, has_side_effects=True, vmem_limit_bytes=56 * 1024 * 1024
        ),
        cost_estimate=pl.CostEstimate(flops=4_000_000_000, bytes_accessed=3_000_000, transcendentals=4_000_000),
    )(
        query_in[0], key_in[0], value_in[0], out_grad[0],
        w_out.reshape(2, w_rows, width), head_offsets, valid_tiles,
    )
    columns = pl.BlockSpec((ROWS, PAIRS * 2 * HD), lambda t: (0, t))
    back = pltpu.with_memory_space_constraint(back, pltpu.VMEM)
    outs = pl.pallas_call(
        finish,
        grid=(HEADS // 2 // PAIRS,),
        out_shape=[jax.ShapeDtypeStruct((ROWS, width), BF16)] * 3,
        in_specs=[smem, pl.BlockSpec(memory_space=pltpu.VMEM)],
        out_specs=[columns] * 3,
    )(head_offsets, back)
    return tuple(o[None] for o in outs)


def solution(mesh):
    rows = P("fsdp", "ctx", None)
    return jax.shard_map(
        on_device,
        mesh=mesh,
        in_specs=(rows, rows, rows, rows, P("fsdp", None), P(), P("fsdp")),
        out_specs=(rows, rows, rows),
        check_vma=False,
    )
```

```python
import jax
import jax.numpy as jnp
from jax import lax
from jax.experimental import pallas as pl
from jax.experimental.pallas import tpu as pltpu
from jax.sharding import PartitionSpec as P

HEADS = 12
HD = 64
GROUP = 8
ROWS = 256
HALF = 128
QUAD = GROUP // 2
SEG = GROUP * HALF
QB = 256
KC = 512
SUB = 256
NEG = -1e30
PAIRS = 3
EARLY = 2
W_CUT = 32
BLOCKS = 6
F32 = jnp.float32
BF16 = jnp.bfloat16
MESH = pl.DeviceIdType.MESH


def nt(a, b):
    return lax.dot_general(a, b, (((1,), (1,)), ((), ())), preferred_element_type=F32)


def nn(a, b):
    return jnp.dot(a, b, preferred_element_type=F32)


def row_perm(value):
    r = lax.broadcasted_iota(jnp.int32, (ROWS, ROWS), 0)
    c = lax.broadcasted_iota(jnp.int32, (ROWS, ROWS), 1)
    pos = jnp.where(r < HALF, 2 * r, 2 * r - (ROWS - 1))
    return jnp.where(c == pos, value, 0.0).astype(BF16)


def row_unperm():
    r = lax.broadcasted_iota(jnp.int32, (ROWS, ROWS), 1)
    c = lax.broadcasted_iota(jnp.int32, (ROWS, ROWS), 0)
    pos = jnp.where(r < HALF, 2 * r, 2 * r - (ROWS - 1))
    return jnp.where(c == pos, 1.0, 0.0).astype(BF16)


def kernel(
    q_in, k_in, v_in, og_in, w_ref, off_ref, valid_ref,
    back,
    xin, qks, vs, gs, qk, vin, gin, vd, kp, kt, w4, ebuf, stat, dpbuf, dsp, acc, xsib, out, og_perm,
    w_send, w_recv, a_send, a_recv, f_send, f_recv, x_send, x_recv, o_send, o_recv,
    l_sem, in_sem, ready,
):
    ctx = lax.axis_index("ctx")
    z = lax.axis_index("fsdp")
    nz = lax.axis_size("fsdp")
    m = ctx % GROUP
    base = ctx - m
    chip = m // 2
    core = m % 2
    half = m // QUAD
    valid = valid_ref[0]

    def dev(member):
        return (base + member, z)

    def remote(src, dst, ssem, rsem, to):
        return pltpu.make_async_remote_copy(
            src_ref=src, dst_ref=dst, send_sem=ssem, recv_sem=rsem, device_id=to, device_id_type=MESH
        )

    def full_head(p):
        return 3 * (p // 2) + 2 * (p % 2)

    upper = z >= nz // 2
    barrier = pltpu.get_barrier_semaphore()
    for dx in range(1, QUAD):
        pl.semaphore_signal(barrier, inc=1, device_id=dev(2 * (chip ^ dx)), device_id_type=MESH)

    @pl.when(jnp.logical_or(core == 1, upper))
    def _():
        pl.semaphore_signal(barrier, inc=1, device_id=dev(m ^ 1), device_id_type=MESH)

    @pl.when(upper)
    def _():
        for dx in range(1, QUAD):
            pl.semaphore_signal(barrier, inc=1, device_id=dev(2 * (chip ^ dx) + 1), device_id_type=MESH)

    for d in (1, 2, nz - 2, nz - 1):
        to = (z + d) % nz
        pl.semaphore_signal(
            barrier, inc=1, device_id=(base + 2 * chip + jnp.where(to >= nz // 2, core, 1), to), device_id_type=MESH
        )
    loads = [pltpu.make_async_copy(x, xin.at[n], in_sem.at[n]) for n, x in enumerate((q_in, k_in, v_in, og_in))]
    for c in loads:
        c.start()
    own_w = pltpu.make_async_copy(w_ref, w4.at[z], l_sem.at[0])
    own_w.start()

    turn = 1 - 2 * core
    pieces = (pl.ds(0, W_CUT), pl.ds(W_CUT, w_ref.shape[1] - W_CUT))

    def w_copy(way, step, n, sender):
        by = turn if way == 0 else -turn
        hop = 2 if step == 4 else 1
        frm = (z - (step - hop if sender else step) * by + nz) % nz
        rows = pieces[n]
        src = w_ref.at[core, rows] if step == 1 else w4.at[frm, core, rows]
        return frm, remote(
            src, w4.at[frm, core, rows], w_send.at[0],
            w_recv.at[(way * 4 + step - 1) * 2 + n], (ctx, (z + hop * by + nz) % nz),
        )

    def arrived(ref, sem):
        pltpu.make_async_copy(ref, ref, sem).wait()

    def w_forward(frm, c):
        return remote(w4.at[frm, c], w4.at[frm, c], w_send.at[1], w_recv.at[16], dev(m ^ 1))

    lane = lax.broadcasted_iota(jnp.int32, (HALF, 2 * HD), 1)
    low = lane < HD

    def takes_odd(tile):
        return jnp.where(low, off_ref[1, 2 * tile], off_ref[1, 2 * tile + 1]) == 1

    def classes(x, odd):
        return jnp.where(odd, x[HALF:], x[:HALF]), jnp.where(odd, x[:HALF], x[HALF:])

    def side_by_side(l, r):
        one = jnp.where(low, l, pltpu.roll(r, HD, 1)).astype(BF16)
        return one, jnp.where(low, pltpu.roll(l, HD, 1), r).astype(BF16)

    def pack_pair(dst, left, right, tile):
        odd = takes_odd(tile)
        for cls, (l, r) in enumerate(zip(classes(left, odd), classes(right, odd))):
            dst[2 * tile, cls], dst[2 * tile + 1, cls] = side_by_side(l, r)

    def pack_one(dst, x, tile):
        dst[2 * tile], dst[2 * tile + 1] = side_by_side(*classes(x, takes_odd(tile)))

    def place(dst, slot, s, to_core):
        s = s ^ (QUAD * to_core)
        return dst.at[slot, :, s] if len(dst.shape) == 5 else dst.at[slot, s]

    def full_copy(src, dst, which, d):
        p = m ^ d
        return remote(
            src.at[full_head(p)], place(dst, 0, m, p % 2), a_send.at[which], a_recv.at[which, 0], dev(p)
        )

    def shared_copy(src, dst, which, dx):
        to = chip ^ dx
        return remote(
            src.at[3 * to + 1], place(dst, 1, m, half), a_send.at[which], a_recv.at[which, 1],
            dev(2 * to + half),
        )

    def local_full(src, dst, which):
        return pltpu.make_async_copy(src.at[full_head(m)], place(dst, 0, m, core), a_recv.at[which, 0])

    def local_shared(src, dst, which):
        return pltpu.make_async_copy(src.at[3 * chip + 1], place(dst, 1, m, half), a_recv.at[which, 1])

    def exchange(src, dst, which, shared_first=False):
        def send_full():
            for d in range(1, GROUP):
                full_copy(src, dst, which, d).start()
            local_full(src, dst, which).start()

        if not shared_first:
            send_full()
        for dx in range(1, QUAD):
            shared_copy(src, dst, which, dx).start()

        @pl.when(core != half)
        def _():
            shared_copy(src, dst, which, 0).start()

        @pl.when(core == half)
        def _():
            local_shared(src, dst, which).start()

        if shared_first:
            send_full()

    def wait_full(dst, which):
        arrived(dst.at[0], a_recv.at[which, 0])

    def wait_shared(dst, which):
        arrived(dst.at[1, :, 0:QUAD] if which == 0 else dst.at[1, 0:QUAD], a_recv.at[which, 1])

    def positions(row, cls, off):
        return base * ROWS + 2 * row + (off if cls == 0 else 1 - off)

    wide = lax.broadcasted_iota(jnp.int32, (KC, 2 * HD), 1)
    key_row = lax.broadcasted_iota(jnp.int32, (KC, 1), 0)

    def prepare(slot, cls, seg, off):
        bias = jnp.where(positions((seg ^ core) * KC + key_row, cls, off) < valid, 0.0, NEG)
        x = qk[slot, cls, seg * QUAD:(seg + 1) * QUAD].reshape(KC, 2 * HD).astype(F32)
        rows = slice(seg * KC, (seg + 1) * KC)
        kp[slot, cls, rows] = jnp.where(wide >= HD, x, jnp.where(wide == 0, bias, 0.0)).astype(BF16)
        kt[slot, cls, :, rows] = jnp.transpose(x)[HD:].astype(BF16)

    def join(slot, cls, seg, with_grad):
        part = slice(seg * QUAD, (seg + 1) * QUAD)
        x = vin[slot, part].reshape(KC, 2 * HD).astype(F32)
        g = 0.0
        if cls:
            x = pltpu.roll(x, HD, 1)
        if with_grad:
            g = gin[slot, part].reshape(KC, 2 * HD).astype(F32)
            if not cls:
                g = pltpu.roll(g, HD, 1)
        vd[slot, cls, part] = jnp.where(wide < HD, x, g).astype(BF16).reshape(QUAD, HALF, 2 * HD)

    qlane = lax.broadcasted_iota(jnp.int32, (QB, 2 * HD), 1)
    qlow = qlane < HD
    qrow = lax.broadcasted_iota(jnp.int32, (QB, 1), 0)

    def fold(x, op):
        return op(x.reshape(SUB // 8, 8, QB), axis=0)

    def chunks_of(c, cls):
        if cls == 0:
            return [(0, 0, c, 2), (1, 0, 1 - c, 1), (2, 1, c, 1)]
        return [(3, 0, c, 1), (4, 1, c, 1)]

    def scores(slot, off, c, i, cls):
        b = 4 * slot + 2 * c + i
        r0 = (c ^ core) * KC + i * QB
        xq = qk[slot, cls, c * QUAD + 2 * i:c * QUAD + 2 * i + 2].reshape(QB, 2 * HD).astype(F32)
        use = jnp.where(positions(r0 + qrow, cls, off) < valid, 1.0, 0.0)
        qp = jnp.where(qlow, jnp.where(qlane == 0, use, 0.0), pltpu.roll(xq, HD, 1)).astype(BF16)
        chunks = chunks_of(c, cls)
        top = jnp.full((8, QB), -jnp.inf, F32)
        for n, kc, seg, mult in chunks:
            for u in range(KC // SUB):
                s = nt(kp[slot, kc, seg * KC + u * SUB:seg * KC + (u + 1) * SUB], qp)
                ebuf[b, n, u * SUB:(u + 1) * SUB] = s
                top = jnp.maximum(top, fold(s, jnp.max))
        top = jnp.max(top, axis=0, keepdims=True)
        total = jnp.zeros((8, QB), F32)
        for n, kc, seg, mult in chunks:
            for u in range(KC // SUB):
                su = slice(u * SUB, (u + 1) * SUB)
                e = jnp.exp(ebuf[b, n, su] - top)
                ebuf[b, n, su] = e
                total = total + mult * fold(e, jnp.sum)
        stat[b, cls] = 1.0 / jnp.sum(total, axis=0, keepdims=True)

    def send_out(slot, c, j, kind):
        j = j ^ (m % QUAD)
        head = full_head(m) if slot == 0 else 3 * chip + 1
        return remote(
            out.at[slot, QUAD * c + j, kind], back.at[head, kind], o_send.at[0], o_recv.at[0],
            dev(QUAD * (c ^ core) + j),
        )

    def start_others(slot, c, kind):
        for j in range(1, QUAD):
            send_out(slot, c, j, kind).start()

    def start_last(slot, c, kinds):
        head = full_head(m) if slot == 0 else 3 * chip + 1

        @pl.when((c ^ core) != half)
        def _():
            for kind in kinds:
                send_out(slot, c, 0, kind).start()

        @pl.when((c ^ core) == half)
        def _():
            for kind in kinds:
                pltpu.make_async_copy(
                    out.at[slot, QUAD * c + m % QUAD, kind], back.at[head, kind], o_recv.at[0]
                ).start()

    def put_terms(slot, cls, c, x):
        out[slot, QUAD * c:QUAD * (c + 1), cls] = x.reshape(QUAD, HALF, 2 * HD).astype(BF16)
        start_others(slot, c, cls)

    def segment(slot, c, order, take):
        rows = {}
        stats = {}
        for cls in range(2):
            for i in range(2):
                b = 4 * slot + 2 * c + i
                s0 = c * QUAD + 2 * i
                xq = qk[slot, cls, s0:s0 + 2].reshape(QB, 2 * HD).astype(F32)
                xv = vd[slot, cls, s0:s0 + 2].reshape(QB, 2 * HD).astype(F32)
                g = jnp.where(qlow, 0.0, xv)
                rows[cls, i] = jnp.concatenate([jnp.where(qlow, xq, 0.0).astype(BF16), g.astype(BF16)], axis=0)
                gp = pltpu.roll(g, HD, 1).astype(BF16)
                dot_sum = jnp.zeros((8, QB), F32)
                for n, kc, seg, mult in chunks_of(c, cls):
                    for u in range(KC // SUB):
                        su = slice(u * SUB, (u + 1) * SUB)
                        per = SUB // HALF
                        s1 = seg * QUAD + u * per
                        dp = nt(vd[slot, kc, s1:s1 + per].reshape(SUB, 2 * HD), gp)
                        dpbuf[i, n, su] = dp
                        dot_sum = dot_sum + mult * fold(ebuf[b, n, su] * dp, jnp.sum)
                inv = stat[b, cls]
                stats[cls, i] = (inv, jnp.sum(dot_sum, axis=0, keepdims=True) * inv)
        dqt = {}
        for kc, seg in order:
            terms = None
            for cls in range(2):
                for n, kn, sn, mult in chunks_of(c, cls):
                    if (kn, sn) != (kc, seg):
                        continue
                    keys_t = kt[slot, kc, :, seg * KC:(seg + 1) * KC]
                    keys_t = keys_t * mult if mult != 1 else keys_t
                    for i in range(2):
                        b = 4 * slot + 2 * c + i
                        inv, delta = stats[cls, i]
                        for u in range(KC // SUB):
                            su = slice(u * SUB, (u + 1) * SUB)
                            p = ebuf[b, n, su] * inv
                            ds = p * (dpbuf[i, n, su] - delta)
                            dsp[i, n, su, :QB] = ds.astype(BF16)
                            dsp[i, n, su, QB:] = p.astype(BF16)
                        g = rows[cls, i] * mult if mult != 1 else rows[cls, i]
                        t = nn(dsp[i, n], g)
                        terms = t if terms is None else terms + t
                        t = nn(keys_t, dsp[i, n, :, :QB])
                        dqt[cls, i] = dqt[cls, i] + t if (cls, i) in dqt else t
            take(kc, seg, terms)
        for i in range(2):
            s0 = QUAD * c + 2 * i
            dq = jnp.transpose(jnp.concatenate([dqt[0, i], dqt[1, i]], axis=0)) * (HD ** -0.5)
            out[slot, s0:s0 + 2, 2] = dq.reshape(2, HALF, 2 * HD).astype(BF16)
        start_others(slot, c, 2)

    first, other = slice(0, QUAD), slice(QUAD, GROUP)

    def pass_on(dst, which):
        src, to = (dst.at[1, 0, first], dst.at[1, 0, other]) if which == 0 else (dst.at[1, first], dst.at[1, other])
        return remote(src, to, f_send.at[which], f_recv.at[which], dev(m ^ 1))

    off0 = off_ref[1, full_head(m)]
    off1 = off_ref[1, 3 * chip + 1]

    def first_w():
        for n in range(2):
            for way in range(2):
                w_copy(way, 1, n, True)[1].start()

    @pl.when(upper)
    def _():
        pl.semaphore_wait(barrier, GROUP - 1 + 4)
        first_w()

    @pl.when(jnp.logical_and(core == 0, jnp.logical_not(upper)))
    def _():
        pl.semaphore_wait(barrier, GROUP - 1)
        pl.semaphore_signal(ready, inc=1, device_id=dev(m ^ 1), device_id_type=MESH)

    perm = row_perm(1.0)
    perm_q = row_perm(HD ** -0.5)
    loads[0].wait()
    loads[1].wait()
    for t in range(HEADS // 2):
        cols = slice(t * 128, (t + 1) * 128)
        pack_pair(qks, nn(perm_q, xin[0, :, cols]), nn(perm, xin[1, :, cols]), t)
    @pl.when(jnp.logical_and(core == 1, jnp.logical_not(upper)))
    def _():
        pl.semaphore_wait(ready, 1)

    exchange(qks, qk, 0)

    @pl.when(jnp.logical_not(upper))
    def _():
        @pl.when(core == 1)
        def _():
            pl.semaphore_wait(barrier, 2 * 4)
            pl.semaphore_signal(ready, inc=1, device_id=dev(m ^ 1), device_id_type=MESH)

        @pl.when(core == 0)
        def _():
            pl.semaphore_wait(ready, 1)

        first_w()

    loads[2].wait()
    for t in range(HEADS // 2):
        pack_one(vs, nn(perm, xin[2, :, t * 128:(t + 1) * 128]), t)
    exchange(vs, vin, 1)

    loads[3].wait()
    og_perm[...] = nn(perm, xin[3]).astype(BF16)
    for step in range(1, 4):
        for n in range(2):
            for way in range(2):
                frm, arrival = w_copy(way, step, n, False)
                arrival.wait_recv()
                if step < 3:
                    w_copy(way, step + 1, n, True)[1].start()
                if step == 2 and n == way:
                    w_copy(way, 4, n, True)[1].start()
                if n == 1:
                    w_forward(frm, core).start()

    wait_full(qk, 0)
    for cls in range(2):
        for seg in range(2):
            prepare(0, cls, seg, off0)

    for t in range(EARLY):
        for cls in range(2):
            scores(0, off0, t // 2, t % 2, cls)

    for way in range(2):
        frm, arrival = w_copy(way, 4, way, False)
        arrival.wait_recv()
    w_forward(frm, core).start()
    own_w.wait()
    arrived(w4.at[pl.ds(0, nz - 1), 0], w_recv.at[16])
    grad = nt(og_perm[...], w4[...].reshape(HEADS * HD, HEADS * HD))
    r = lax.broadcasted_iota(jnp.int32, (ROWS, 1), 0)
    position = ctx * ROWS + jnp.where(r < HALF, 2 * r, 2 * r - (ROWS - 1))
    grad = jnp.where(position < valid, grad, 0.0)
    for t in range(HEADS // 2):
        cols = slice(t * 128, (t + 1) * 128)
        pack_one(gs, grad[:, cols], t)
    exchange(gs, gin, 2, shared_first=True)

    wait_shared(qk, 0)
    pass_on(qk, 0).start()

    for t in range(EARLY, 4):
        for cls in range(2):
            scores(0, off0, t // 2, t % 2, cls)

    pass_on(qk, 0).wait_recv()
    prepare(1, 0, 0, off1)
    prepare(1, 0, 1, off1)
    prepare(1, 1, 0, off1)
    wait_shared(vin, 1)
    pass_on(vin, 1).start()

    for t in range(2):
        for cls in range(2):
            scores(1, off1, 0, t, cls)

    swap_terms = remote(acc.at[0], xsib, x_send.at[0], x_recv.at[0], dev(m ^ 1))

    def take_shared(kc, seg, x):
        if kc:
            put_terms(1, 1, 0, x)
        elif seg:
            acc[0] = x
            swap_terms.start()
        else:
            swap_terms.wait_recv()
            put_terms(1, 0, 0, x + xsib[...])

    def take_first(kc, seg, x):
        if kc:
            put_terms(0, 1, 0, x)
        else:
            acc[1 + seg] = x

    def take_second(kc, seg, x):
        put_terms(0, kc, seg, x if kc else x + acc[1 + seg])

    pass_on(vin, 1).wait_recv()
    join(1, 0, 1, False)
    wait_shared(gin, 2)
    join(1, 0, 0, True)
    join(1, 1, 0, True)
    segment(1, 0, ((0, 1), (1, 0), (0, 0)), take_shared)
    start_last(1, 0, (1, 0, 2))

    wait_full(vin, 1)
    wait_full(gin, 2)
    for cls in range(2):
        for c in range(2):
            join(0, cls, c, True)
    segment(0, 0, ((1, 0), (0, 0), (0, 1)), take_first)
    start_last(0, 0, (1, 2))
    segment(0, 1, ((0, 0), (0, 1), (1, 1)), take_second)
    start_last(0, 0, (0,))
    start_last(0, 1, (0, 1, 2))

    arrived(back, o_recv.at[0])

    arrived(w4.at[pl.ds(0, nz - 1), 0], w_send.at[0])
    arrived(w4.at[pl.ds(0, nz - 1), 0], w_send.at[1])
    swap_terms.wait_send()
    pass_on(qk, 0).wait_send()
    pass_on(vin, 1).wait_send()

    def all_left(blocks):
        for which, src in enumerate((qks, vs, gs)):
            arrived(src.at[pl.ds(0, blocks)], a_send.at[which])
        arrived(back.at[pl.ds(0, blocks)], o_send.at[0])

    @pl.when(core != half)
    def _():
        all_left(GROUP - 1 + QUAD)

    @pl.when(core == half)
    def _():
        all_left(GROUP - 1 + QUAD - 1)


def finish(off_ref, back, dq_ref, dk_ref, dv_ref):
    lane = lax.broadcasted_iota(jnp.int32, (HALF, 2 * HD), 1)
    low = lane < HD
    unperm = row_unperm()
    first = pl.program_id(0) * PAIRS
    for t in range(PAIRS):
        cols = slice(t * 128, (t + 1) * 128)
        odd = jnp.where(low, off_ref[1, 2 * (first + t)], off_ref[1, 2 * (first + t) + 1]) == 1

        def put(ref, sel, oth):
            rows = jnp.concatenate([jnp.where(odd, oth, sel), jnp.where(odd, sel, oth)], axis=0)
            ref[:, cols] = nn(unperm, rows.astype(BF16)).astype(BF16)

        one = [back[2 * (first + t), n].astype(F32) for n in range(3)]
        two = [back[2 * (first + t) + 1, n].astype(F32) for n in range(3)]
        left = [jnp.where(low, one[n], pltpu.roll(two[n], HD, 1)) for n in range(3)]
        right = [jnp.where(low, pltpu.roll(one[n], HD, 1), two[n]) for n in range(3)]
        put(dk_ref, left[0], left[1])
        put(dv_ref, right[0], right[1])
        put(dq_ref, left[2], right[2])


def on_device(query_in, key_in, value_in, out_grad, w_out, head_offsets, valid_tiles):
    width = HEADS * HD
    nz = lax.axis_size("fsdp")
    w_rows = w_out.shape[0] // 2
    far = pl.BlockSpec(memory_space=pl.ANY)
    smem = pl.BlockSpec(memory_space=pltpu.SMEM)
    dma = pltpu.SemaphoreType.DMA
    back = pl.pallas_call(
        kernel,
        out_shape=pltpu.VMEM((HEADS, 3, HALF, 2 * HD), BF16),
        in_specs=[far] * 5 + [smem] * 2,
        out_specs=pl.BlockSpec(memory_space=pltpu.VMEM),
        scratch_shapes=[
            pltpu.VMEM((4, ROWS, width), BF16),
            pltpu.VMEM((HEADS, 2, HALF, 2 * HD), BF16),
            pltpu.VMEM((HEADS, HALF, 2 * HD), BF16),
            pltpu.VMEM((HEADS, HALF, 2 * HD), BF16),
            pltpu.VMEM((2, 2, GROUP, HALF, 2 * HD), BF16),
            pltpu.VMEM((2, GROUP, HALF, 2 * HD), BF16),
            pltpu.VMEM((2, GROUP, HALF, 2 * HD), BF16),
            pltpu.VMEM((2, 2, GROUP, HALF, 2 * HD), BF16),
            pltpu.VMEM((2, 2, SEG, 2 * HD), BF16),
            pltpu.VMEM((2, 2, HD, SEG), BF16),
            pltpu.VMEM((nz, 2, w_rows, width), BF16),
            pltpu.VMEM((BLOCKS, 5, KC, QB), F32),
            pltpu.VMEM((BLOCKS, 2, 1, QB), F32),
            pltpu.VMEM((2, 5, KC, QB), F32),
            pltpu.VMEM((2, 5, KC, 2 * QB), BF16),
            pltpu.VMEM((3, KC, 2 * HD), F32),
            pltpu.VMEM((KC, 2 * HD), F32),
            pltpu.VMEM((2, GROUP, 3, HALF, 2 * HD), BF16),
            pltpu.VMEM((ROWS, width), BF16),
            dma((2,)), dma((17,)), dma((3,)), dma((3, 2)),
            dma((2,)), dma((2,)), dma((1,)), dma((1,)), dma((1,)), dma((1,)), dma((1,)), dma((4,)),
            pltpu.SemaphoreType.REGULAR,
        ],
        compiler_params=pltpu.CompilerParams(
            collective_id=0, has_side_effects=True, vmem_limit_bytes=56 * 1024 * 1024
        ),
        cost_estimate=pl.CostEstimate(flops=4_000_000_000, bytes_accessed=3_000_000, transcendentals=4_000_000),
    )(
        query_in[0], key_in[0], value_in[0], out_grad[0],
        w_out.reshape(2, w_rows, width), head_offsets, valid_tiles,
    )
    columns = pl.BlockSpec((ROWS, PAIRS * 2 * HD), lambda t: (0, t))
    back = pltpu.with_memory_space_constraint(back, pltpu.VMEM)
    outs = pl.pallas_call(
        finish,
        grid=(HEADS // 2 // PAIRS,),
        out_shape=[jax.ShapeDtypeStruct((ROWS, width), BF16)] * 3,
        in_specs=[smem, pl.BlockSpec(memory_space=pltpu.VMEM)],
        out_specs=[columns] * 3,
    )(head_offsets, back)
    return tuple(o[None] for o in outs)


def solution(mesh):
    rows = P("fsdp", "ctx", None)
    return jax.shard_map(
        on_device,
        mesh=mesh,
        in_specs=(rows, rows, rows, rows, P("fsdp", None), P(), P("fsdp")),
        out_specs=(rows, rows, rows),
        check_vma=False,
    )
```

```python
import jax
import jax.numpy as jnp
from jax import lax
from jax.experimental import pallas as pl
from jax.experimental.pallas import tpu as pltpu
from jax.sharding import PartitionSpec as P

HEADS = 12
HD = 64
GROUP = 8
ROWS = 256
HALF = 128
QUAD = GROUP // 2
SEG = GROUP * HALF
QB = 256
KC = 512
SUB = 256
NEG = -1e30
PAIRS = 6
EARLY = 1
W_CUT = 32
BLOCKS = 6
F32 = jnp.float32
BF16 = jnp.bfloat16
MESH = pl.DeviceIdType.MESH


def nt(a, b):
    return lax.dot_general(a, b, (((1,), (1,)), ((), ())), preferred_element_type=F32)


def nn(a, b):
    return jnp.dot(a, b, preferred_element_type=F32)


def row_perm(value):
    r = lax.broadcasted_iota(jnp.int32, (ROWS, ROWS), 0)
    c = lax.broadcasted_iota(jnp.int32, (ROWS, ROWS), 1)
    pos = jnp.where(r < HALF, 2 * r, 2 * r - (ROWS - 1))
    return jnp.where(c == pos, value, 0.0).astype(BF16)


def row_unperm():
    r = lax.broadcasted_iota(jnp.int32, (ROWS, ROWS), 1)
    c = lax.broadcasted_iota(jnp.int32, (ROWS, ROWS), 0)
    pos = jnp.where(r < HALF, 2 * r, 2 * r - (ROWS - 1))
    return jnp.where(c == pos, 1.0, 0.0).astype(BF16)


def kernel(
    q_in, k_in, v_in, og_in, w_ref, off_ref, valid_ref,
    back,
    xin, qks, vs, gs, qk, vin, gin, vd, kp, kt, w4, ebuf, stat, dpbuf, dsp, acc, xsib, out, og_perm,
    w_send, w_recv, a_send, a_recv, f_send, f_recv, x_send, x_recv, o_send, o_recv,
    l_sem, in_sem, ready,
):
    ctx = lax.axis_index("ctx")
    z = lax.axis_index("fsdp")
    nz = lax.axis_size("fsdp")
    m = ctx % GROUP
    base = ctx - m
    chip = m // 2
    core = m % 2
    half = m // QUAD
    valid = valid_ref[0]

    def dev(member):
        return (base + member, z)

    def remote(src, dst, ssem, rsem, to):
        return pltpu.make_async_remote_copy(
            src_ref=src, dst_ref=dst, send_sem=ssem, recv_sem=rsem, device_id=to, device_id_type=MESH
        )

    def full_head(p):
        return 3 * (p // 2) + 2 * (p % 2)

    upper = z >= nz // 2
    barrier = pltpu.get_barrier_semaphore()
    for dx in range(1, QUAD):
        pl.semaphore_signal(barrier, inc=1, device_id=dev(2 * (chip ^ dx)), device_id_type=MESH)

    @pl.when(jnp.logical_or(core == 1, upper))
    def _():
        pl.semaphore_signal(barrier, inc=1, device_id=dev(m ^ 1), device_id_type=MESH)

    @pl.when(upper)
    def _():
        for dx in range(1, QUAD):
            pl.semaphore_signal(barrier, inc=1, device_id=dev(2 * (chip ^ dx) + 1), device_id_type=MESH)

    for d in (1, 2, nz - 2, nz - 1):
        to = (z + d) % nz
        pl.semaphore_signal(
            barrier, inc=1, device_id=(base + 2 * chip + jnp.where(to >= nz // 2, core, 1), to), device_id_type=MESH
        )
    loads = [pltpu.make_async_copy(x, xin.at[n], in_sem.at[n]) for n, x in enumerate((q_in, k_in, v_in, og_in))]
    for c in loads:
        c.start()
    own_w = pltpu.make_async_copy(w_ref, w4.at[z], l_sem.at[0])
    own_w.start()

    turn = 1 - 2 * core
    pieces = (pl.ds(0, W_CUT), pl.ds(W_CUT, w_ref.shape[1] - W_CUT))

    def w_copy(way, step, n, sender):
        by = turn if way == 0 else -turn
        hop = 2 if step == 4 else 1
        frm = (z - (step - hop if sender else step) * by + nz) % nz
        rows = pieces[n]
        src = w_ref.at[core, rows] if step == 1 else w4.at[frm, core, rows]
        return frm, remote(
            src, w4.at[frm, core, rows], w_send.at[0],
            w_recv.at[(way * 4 + step - 1) * 2 + n], (ctx, (z + hop * by + nz) % nz),
        )

    def arrived(ref, sem):
        pltpu.make_async_copy(ref, ref, sem).wait()

    def w_forward(frm, c):
        return remote(w4.at[frm, c], w4.at[frm, c], w_send.at[1], w_recv.at[16], dev(m ^ 1))

    lane = lax.broadcasted_iota(jnp.int32, (HALF, 2 * HD), 1)
    low = lane < HD

    def takes_odd(tile):
        return jnp.where(low, off_ref[1, 2 * tile], off_ref[1, 2 * tile + 1]) == 1

    def classes(x, odd):
        return jnp.where(odd, x[HALF:], x[:HALF]), jnp.where(odd, x[:HALF], x[HALF:])

    def side_by_side(l, r):
        one = jnp.where(low, l, pltpu.roll(r, HD, 1)).astype(BF16)
        return one, jnp.where(low, pltpu.roll(l, HD, 1), r).astype(BF16)

    def pack_pair(dst, left, right, tile):
        odd = takes_odd(tile)
        for cls, (l, r) in enumerate(zip(classes(left, odd), classes(right, odd))):
            dst[2 * tile, cls], dst[2 * tile + 1, cls] = side_by_side(l, r)

    def pack_one(dst, x, tile):
        dst[2 * tile], dst[2 * tile + 1] = side_by_side(*classes(x, takes_odd(tile)))

    def place(dst, slot, s, to_core):
        s = s ^ (QUAD * to_core)
        return dst.at[slot, :, s] if len(dst.shape) == 5 else dst.at[slot, s]

    def full_copy(src, dst, which, d):
        p = m ^ d
        return remote(
            src.at[full_head(p)], place(dst, 0, m, p % 2), a_send.at[which], a_recv.at[which, 0], dev(p)
        )

    def shared_copy(src, dst, which, dx):
        to = chip ^ dx
        return remote(
            src.at[3 * to + 1], place(dst, 1, m, half), a_send.at[which], a_recv.at[which, 1],
            dev(2 * to + half),
        )

    def local_full(src, dst, which):
        return pltpu.make_async_copy(src.at[full_head(m)], place(dst, 0, m, core), a_recv.at[which, 0])

    def local_shared(src, dst, which):
        return pltpu.make_async_copy(src.at[3 * chip + 1], place(dst, 1, m, half), a_recv.at[which, 1])

    def exchange(src, dst, which, shared_first=False):
        def send_full():
            for d in range(1, GROUP):
                full_copy(src, dst, which, d).start()
            local_full(src, dst, which).start()

        if not shared_first:
            send_full()
        for dx in range(1, QUAD):
            shared_copy(src, dst, which, dx).start()

        @pl.when(core != half)
        def _():
            shared_copy(src, dst, which, 0).start()

        @pl.when(core == half)
        def _():
            local_shared(src, dst, which).start()

        if shared_first:
            send_full()

    def wait_full(dst, which):
        arrived(dst.at[0], a_recv.at[which, 0])

    def wait_shared(dst, which):
        arrived(dst.at[1, :, 0:QUAD] if which == 0 else dst.at[1, 0:QUAD], a_recv.at[which, 1])

    def positions(row, cls, off):
        return base * ROWS + 2 * row + (off if cls == 0 else 1 - off)

    wide = lax.broadcasted_iota(jnp.int32, (KC, 2 * HD), 1)
    key_row = lax.broadcasted_iota(jnp.int32, (KC, 1), 0)

    def prepare(slot, cls, seg, off):
        bias = jnp.where(positions((seg ^ core) * KC + key_row, cls, off) < valid, 0.0, NEG)
        x = qk[slot, cls, seg * QUAD:(seg + 1) * QUAD].reshape(KC, 2 * HD).astype(F32)
        rows = slice(seg * KC, (seg + 1) * KC)
        kp[slot, cls, rows] = jnp.where(wide >= HD, x, jnp.where(wide == 0, bias, 0.0)).astype(BF16)
        kt[slot, cls, :, rows] = jnp.transpose(x)[HD:].astype(BF16)

    def join(slot, cls, seg, with_grad):
        part = slice(seg * QUAD, (seg + 1) * QUAD)
        x = vin[slot, part].reshape(KC, 2 * HD).astype(F32)
        g = 0.0
        if cls:
            x = pltpu.roll(x, HD, 1)
        if with_grad:
            g = gin[slot, part].reshape(KC, 2 * HD).astype(F32)
            if not cls:
                g = pltpu.roll(g, HD, 1)
        vd[slot, cls, part] = jnp.where(wide < HD, x, g).astype(BF16).reshape(QUAD, HALF, 2 * HD)

    qlane = lax.broadcasted_iota(jnp.int32, (QB, 2 * HD), 1)
    qlow = qlane < HD
    qrow = lax.broadcasted_iota(jnp.int32, (QB, 1), 0)

    def fold(x, op):
        return op(x.reshape(SUB // 8, 8, QB), axis=0)

    def chunks_of(c, cls):
        if cls == 0:
            return [(0, 0, c, 2), (1, 0, 1 - c, 1), (2, 1, c, 1)]
        return [(3, 0, c, 1), (4, 1, c, 1)]

    def scores(slot, off, c, i, cls):
        b = 4 * slot + 2 * c + i
        r0 = (c ^ core) * KC + i * QB
        xq = qk[slot, cls, c * QUAD + 2 * i:c * QUAD + 2 * i + 2].reshape(QB, 2 * HD).astype(F32)
        use = jnp.where(positions(r0 + qrow, cls, off) < valid, 1.0, 0.0)
        qp = jnp.where(qlow, jnp.where(qlane == 0, use, 0.0), pltpu.roll(xq, HD, 1)).astype(BF16)
        chunks = chunks_of(c, cls)
        top = jnp.full((8, QB), -jnp.inf, F32)
        for n, kc, seg, mult in chunks:
            for u in range(KC // SUB):
                s = nt(kp[slot, kc, seg * KC + u * SUB:seg * KC + (u + 1) * SUB], qp)
                ebuf[b, n, u * SUB:(u + 1) * SUB] = s
                top = jnp.maximum(top, fold(s, jnp.max))
        top = jnp.max(top, axis=0, keepdims=True)
        total = jnp.zeros((8, QB), F32)
        for n, kc, seg, mult in chunks:
            for u in range(KC // SUB):
                su = slice(u * SUB, (u + 1) * SUB)
                e = jnp.exp(ebuf[b, n, su] - top)
                ebuf[b, n, su] = e
                total = total + mult * fold(e, jnp.sum)
        stat[b, cls] = 1.0 / jnp.sum(total, axis=0, keepdims=True)

    def send_out(slot, c, j, kind):
        j = j ^ (m % QUAD)
        head = full_head(m) if slot == 0 else 3 * chip + 1
        return remote(
            out.at[slot, QUAD * c + j, kind], back.at[head, kind], o_send.at[0], o_recv.at[0],
            dev(QUAD * (c ^ core) + j),
        )

    def start_others(slot, c, kind):
        for j in range(1, QUAD):
            send_out(slot, c, j, kind).start()

    def start_last(slot, c, kinds):
        head = full_head(m) if slot == 0 else 3 * chip + 1

        @pl.when((c ^ core) != half)
        def _():
            for kind in kinds:
                send_out(slot, c, 0, kind).start()

        @pl.when((c ^ core) == half)
        def _():
            for kind in kinds:
                pltpu.make_async_copy(
                    out.at[slot, QUAD * c + m % QUAD, kind], back.at[head, kind], o_recv.at[0]
                ).start()

    def put_terms(slot, cls, c, x):
        out[slot, QUAD * c:QUAD * (c + 1), cls] = x.reshape(QUAD, HALF, 2 * HD).astype(BF16)
        start_others(slot, c, cls)

    def segment(slot, c, order, take):
        rows = {}
        stats = {}
        for cls in range(2):
            for i in range(2):
                b = 4 * slot + 2 * c + i
                s0 = c * QUAD + 2 * i
                xq = qk[slot, cls, s0:s0 + 2].reshape(QB, 2 * HD).astype(F32)
                xv = vd[slot, cls, s0:s0 + 2].reshape(QB, 2 * HD).astype(F32)
                g = jnp.where(qlow, 0.0, xv)
                rows[cls, i] = jnp.concatenate([jnp.where(qlow, xq, 0.0).astype(BF16), g.astype(BF16)], axis=0)
                gp = pltpu.roll(g, HD, 1).astype(BF16)
                dot_sum = jnp.zeros((8, QB), F32)
                for n, kc, seg, mult in chunks_of(c, cls):
                    for u in range(KC // SUB):
                        su = slice(u * SUB, (u + 1) * SUB)
                        per = SUB // HALF
                        s1 = seg * QUAD + u * per
                        dp = nt(vd[slot, kc, s1:s1 + per].reshape(SUB, 2 * HD), gp)
                        dpbuf[i, n, su] = dp
                        dot_sum = dot_sum + mult * fold(ebuf[b, n, su] * dp, jnp.sum)
                inv = stat[b, cls]
                stats[cls, i] = (inv, jnp.sum(dot_sum, axis=0, keepdims=True) * inv)
        dqt = {}
        for kc, seg in order:
            terms = None
            for cls in range(2):
                for n, kn, sn, mult in chunks_of(c, cls):
                    if (kn, sn) != (kc, seg):
                        continue
                    keys_t = kt[slot, kc, :, seg * KC:(seg + 1) * KC]
                    keys_t = keys_t * mult if mult != 1 else keys_t
                    for i in range(2):
                        b = 4 * slot + 2 * c + i
                        inv, delta = stats[cls, i]
                        for u in range(KC // SUB):
                            su = slice(u * SUB, (u + 1) * SUB)
                            p = ebuf[b, n, su] * inv
                            ds = p * (dpbuf[i, n, su] - delta)
                            dsp[i, n, su, :QB] = ds.astype(BF16)
                            dsp[i, n, su, QB:] = p.astype(BF16)
                        g = rows[cls, i] * mult if mult != 1 else rows[cls, i]
                        t = nn(dsp[i, n], g)
                        terms = t if terms is None else terms + t
                        t = nn(keys_t, dsp[i, n, :, :QB])
                        dqt[cls, i] = dqt[cls, i] + t if (cls, i) in dqt else t
            take(kc, seg, terms)
        for i in range(2):
            s0 = QUAD * c + 2 * i
            dq = jnp.transpose(jnp.concatenate([dqt[0, i], dqt[1, i]], axis=0)) * (HD ** -0.5)
            out[slot, s0:s0 + 2, 2] = dq.reshape(2, HALF, 2 * HD).astype(BF16)
        start_others(slot, c, 2)

    first, other = slice(0, QUAD), slice(QUAD, GROUP)

    def pass_on(dst, which):
        src, to = (dst.at[1, 0, first], dst.at[1, 0, other]) if which == 0 else (dst.at[1, first], dst.at[1, other])
        return remote(src, to, f_send.at[which], f_recv.at[which], dev(m ^ 1))

    off0 = off_ref[1, full_head(m)]
    off1 = off_ref[1, 3 * chip + 1]

    def first_w():
        for n in range(2):
            for way in range(2):
                w_copy(way, 1, n, True)[1].start()

    @pl.when(upper)
    def _():
        pl.semaphore_wait(barrier, GROUP - 1 + 4)
        first_w()

    @pl.when(jnp.logical_and(core == 0, jnp.logical_not(upper)))
    def _():
        pl.semaphore_wait(barrier, GROUP - 1)
        pl.semaphore_signal(ready, inc=1, device_id=dev(m ^ 1), device_id_type=MESH)

    perm = row_perm(1.0)
    perm_q = row_perm(HD ** -0.5)
    loads[0].wait()
    loads[1].wait()
    for t in range(HEADS // 2):
        cols = slice(t * 128, (t + 1) * 128)
        pack_pair(qks, nn(perm_q, xin[0, :, cols]), nn(perm, xin[1, :, cols]), t)
    @pl.when(jnp.logical_and(core == 1, jnp.logical_not(upper)))
    def _():
        pl.semaphore_wait(ready, 1)

    exchange(qks, qk, 0)

    @pl.when(jnp.logical_not(upper))
    def _():
        @pl.when(core == 1)
        def _():
            pl.semaphore_wait(barrier, 2 * 4)
            pl.semaphore_signal(ready, inc=1, device_id=dev(m ^ 1), device_id_type=MESH)

        @pl.when(core == 0)
        def _():
            pl.semaphore_wait(ready, 1)

        first_w()

    loads[2].wait()
    for t in range(HEADS // 2):
        pack_one(vs, nn(perm, xin[2, :, t * 128:(t + 1) * 128]), t)
    exchange(vs, vin, 1)

    loads[3].wait()
    og_perm[...] = nn(perm, xin[3]).astype(BF16)
    for step in range(1, 4):
        for n in range(2):
            for way in range(2):
                frm, arrival = w_copy(way, step, n, False)
                arrival.wait_recv()
                if step < 3:
                    w_copy(way, step + 1, n, True)[1].start()
                if step == 2 and n == way:
                    w_copy(way, 4, n, True)[1].start()
                if n == 1:
                    w_forward(frm, core).start()

    wait_full(qk, 0)
    for cls in range(2):
        for seg in range(2):
            prepare(0, cls, seg, off0)

    for t in range(EARLY):
        for cls in range(2):
            scores(0, off0, t // 2, t % 2, cls)

    for way in range(2):
        frm, arrival = w_copy(way, 4, way, False)
        arrival.wait_recv()
    w_forward(frm, core).start()
    own_w.wait()
    arrived(w4.at[pl.ds(0, nz - 1), 0], w_recv.at[16])
    grad = nt(og_perm[...], w4[...].reshape(HEADS * HD, HEADS * HD))
    r = lax.broadcasted_iota(jnp.int32, (ROWS, 1), 0)
    position = ctx * ROWS + jnp.where(r < HALF, 2 * r, 2 * r - (ROWS - 1))
    grad = jnp.where(position < valid, grad, 0.0)
    for t in range(HEADS // 2):
        cols = slice(t * 128, (t + 1) * 128)
        pack_one(gs, grad[:, cols], t)
    exchange(gs, gin, 2, shared_first=True)

    wait_shared(qk, 0)
    pass_on(qk, 0).start()

    for t in range(EARLY, 4):
        for cls in range(2):
            scores(0, off0, t // 2, t % 2, cls)

    pass_on(qk, 0).wait_recv()
    prepare(1, 0, 0, off1)
    prepare(1, 0, 1, off1)
    prepare(1, 1, 0, off1)
    wait_shared(vin, 1)
    pass_on(vin, 1).start()

    for t in range(2):
        for cls in range(2):
            scores(1, off1, 0, t, cls)

    swap_terms = remote(acc.at[0], xsib, x_send.at[0], x_recv.at[0], dev(m ^ 1))

    def take_shared(kc, seg, x):
        if kc:
            put_terms(1, 1, 0, x)
        elif seg:
            acc[0] = x
            swap_terms.start()
        else:
            swap_terms.wait_recv()
            put_terms(1, 0, 0, x + xsib[...])

    def take_first(kc, seg, x):
        if kc:
            put_terms(0, 1, 0, x)
        else:
            acc[1 + seg] = x

    def take_second(kc, seg, x):
        put_terms(0, kc, seg, x if kc else x + acc[1 + seg])

    pass_on(vin, 1).wait_recv()
    join(1, 0, 1, False)
    wait_shared(gin, 2)
    join(1, 0, 0, True)
    join(1, 1, 0, True)
    segment(1, 0, ((1, 0), (0, 1), (0, 0)), take_shared)
    start_last(1, 0, (1, 0, 2))

    wait_full(vin, 1)
    wait_full(gin, 2)
    for cls in range(2):
        for c in range(2):
            join(0, cls, c, True)
    segment(0, 0, ((1, 0), (0, 0), (0, 1)), take_first)
    start_last(0, 0, (1, 2))
    segment(0, 1, ((0, 0), (0, 1), (1, 1)), take_second)
    start_last(0, 0, (0,))
    start_last(0, 1, (0, 1, 2))

    arrived(back, o_recv.at[0])

    arrived(w4.at[pl.ds(0, nz - 1), 0], w_send.at[0])
    arrived(w4.at[pl.ds(0, nz - 1), 0], w_send.at[1])
    swap_terms.wait_send()
    pass_on(qk, 0).wait_send()
    pass_on(vin, 1).wait_send()

    def all_left(blocks):
        for which, src in enumerate((qks, vs, gs)):
            arrived(src.at[pl.ds(0, blocks)], a_send.at[which])
        arrived(back.at[pl.ds(0, blocks)], o_send.at[0])

    @pl.when(core != half)
    def _():
        all_left(GROUP - 1 + QUAD)

    @pl.when(core == half)
    def _():
        all_left(GROUP - 1 + QUAD - 1)


def finish(off_ref, back, dq_ref, dk_ref, dv_ref):
    lane = lax.broadcasted_iota(jnp.int32, (HALF, 2 * HD), 1)
    low = lane < HD
    unperm = row_unperm()
    first = pl.program_id(0) * PAIRS
    for t in range(PAIRS):
        cols = slice(t * 128, (t + 1) * 128)
        odd = jnp.where(low, off_ref[1, 2 * (first + t)], off_ref[1, 2 * (first + t) + 1]) == 1

        def put(ref, sel, oth):
            rows = jnp.concatenate([jnp.where(odd, oth, sel), jnp.where(odd, sel, oth)], axis=0)
            ref[:, cols] = nn(unperm, rows.astype(BF16)).astype(BF16)

        one = [back[2 * (first + t), n].astype(F32) for n in range(3)]
        two = [back[2 * (first + t) + 1, n].astype(F32) for n in range(3)]
        left = [jnp.where(low, one[n], pltpu.roll(two[n], HD, 1)) for n in range(3)]
        right = [jnp.where(low, pltpu.roll(one[n], HD, 1), two[n]) for n in range(3)]
        put(dk_ref, left[0], left[1])
        put(dv_ref, right[0], right[1])
        put(dq_ref, left[2], right[2])


def on_device(query_in, key_in, value_in, out_grad, w_out, head_offsets, valid_tiles):
    width = HEADS * HD
    nz = lax.axis_size("fsdp")
    w_rows = w_out.shape[0] // 2
    far = pl.BlockSpec(memory_space=pl.ANY)
    smem = pl.BlockSpec(memory_space=pltpu.SMEM)
    dma = pltpu.SemaphoreType.DMA
    back = pl.pallas_call(
        kernel,
        out_shape=pltpu.VMEM((HEADS, 3, HALF, 2 * HD), BF16),
        in_specs=[far] * 5 + [smem] * 2,
        out_specs=pl.BlockSpec(memory_space=pltpu.VMEM),
        scratch_shapes=[
            pltpu.VMEM((4, ROWS, width), BF16),
            pltpu.VMEM((HEADS, 2, HALF, 2 * HD), BF16),
            pltpu.VMEM((HEADS, HALF, 2 * HD), BF16),
            pltpu.VMEM((HEADS, HALF, 2 * HD), BF16),
            pltpu.VMEM((2, 2, GROUP, HALF, 2 * HD), BF16),
            pltpu.VMEM((2, GROUP, HALF, 2 * HD), BF16),
            pltpu.VMEM((2, GROUP, HALF, 2 * HD), BF16),
            pltpu.VMEM((2, 2, GROUP, HALF, 2 * HD), BF16),
            pltpu.VMEM((2, 2, SEG, 2 * HD), BF16),
            pltpu.VMEM((2, 2, HD, SEG), BF16),
            pltpu.VMEM((nz, 2, w_rows, width), BF16),
            pltpu.VMEM((BLOCKS, 5, KC, QB), F32),
            pltpu.VMEM((BLOCKS, 2, 1, QB), F32),
            pltpu.VMEM((2, 5, KC, QB), F32),
            pltpu.VMEM((2, 5, KC, 2 * QB), BF16),
            pltpu.VMEM((3, KC, 2 * HD), F32),
            pltpu.VMEM((KC, 2 * HD), F32),
            pltpu.VMEM((2, GROUP, 3, HALF, 2 * HD), BF16),
            pltpu.VMEM((ROWS, width), BF16),
            dma((2,)), dma((17,)), dma((3,)), dma((3, 2)),
            dma((2,)), dma((2,)), dma((1,)), dma((1,)), dma((1,)), dma((1,)), dma((1,)), dma((4,)),
            pltpu.SemaphoreType.REGULAR,
        ],
        compiler_params=pltpu.CompilerParams(
            collective_id=0, has_side_effects=True, vmem_limit_bytes=56 * 1024 * 1024
        ),
        cost_estimate=pl.CostEstimate(flops=4_000_000_000, bytes_accessed=3_000_000, transcendentals=4_000_000),
    )(
        query_in[0], key_in[0], value_in[0], out_grad[0],
        w_out.reshape(2, w_rows, width), head_offsets, valid_tiles,
    )
    columns = pl.BlockSpec((ROWS, PAIRS * 2 * HD), lambda t: (0, t))
    back = pltpu.with_memory_space_constraint(back, pltpu.VMEM)
    outs = pl.pallas_call(
        finish,
        grid=(HEADS // 2 // PAIRS,),
        out_shape=[jax.ShapeDtypeStruct((ROWS, width), BF16)] * 3,
        in_specs=[smem, pl.BlockSpec(memory_space=pltpu.VMEM)],
        out_specs=[columns] * 3,
    )(head_offsets, back)
    return tuple(o[None] for o in outs)


def solution(mesh):
    rows = P("fsdp", "ctx", None)
    return jax.shard_map(
        on_device,
        mesh=mesh,
        in_specs=(rows, rows, rows, rows, P("fsdp", None), P(), P("fsdp")),
        out_specs=(rows, rows, rows),
        check_vma=False,
    )
```
